32 devices in a mesh: section: 4 (over y, core), row: 4 (over z), col: 2 (over x).
Axes of the slice: x: 2, y: 2, z: 4, core: 2. Of those that a mesh axis runs over, the one named last changes fastest.
Arguments:
- inputs: bfloat16 [4, 768, 5120], P('section', 'row', 'col'), may hold values from -12 to 12
- down_weight: bfloat16 [4, 512, 5120], P('section', 'row', 'col'), may hold values from -5 to 5
- up_weight: bfloat16 [4, 512, 8192], P('section', 'row', 'col'), may hold values from -0.25 to 0.25
- value_grad: bfloat16 [4, 768, 8192], P('section', 'row', 'col'), may hold values from -1.1953125 to 1.1953125
Outputs:
- passed_grad: bfloat16 [4, 768, 5120], P('section', 'row', 'col')
- down_grad: bfloat16 [4, 512, 5120], P('section', 'row', 'col')
- up_grad: bfloat16 [4, 512, 8192], P('section', 'row', 'col')
The draws below stay inside these ranges and needn't reach their ends.
All inputs are finite; a program needn't handle non-finite values.
Results may differ from the reference program's by a relative error of at most 0.03.
Values may be sent and summed in bfloat16 or wider, within the bound.
No kernel may reach another device: no remote copies, remote signals or barrier semaphores. Data moves between devices by JAX's collectives and lax.ppermute only.
A program may use at most 64 MiB of HBM per device.

```python
import math
import jax
import jax.numpy as jnp
from jax import lax

D = 5120
L = 512
TOK_ROW = 192
TOKENS = 768
FEAT = 8192
SEGMENTS = 4
N_ROW = 4


def draw_inputs(key, part):
    first, second = jax.random.split(key, 2)
    scales = jnp.exp(jax.random.uniform(first, (SEGMENTS, TOKENS, 1), jnp.float32, math.log(0.3), math.log(3.0)))
    values = jnp.clip(jax.random.normal(second, (SEGMENTS, TOKENS, D), jnp.float32), -4.0, 4.0)
    return (values * scales).astype(jnp.bfloat16)


def draw_down_weight(key, part):
    first, second = jax.random.split(key, 2)
    scales = jnp.exp(jax.random.uniform(first, (SEGMENTS, L, 1), jnp.float32, 0.0, math.log(10.0)))
    values = jnp.clip(jax.random.normal(second, (SEGMENTS, L, D), jnp.float32), -4.0, 4.0)
    return (values * scales * (1.0 / math.sqrt(D))).astype(jnp.bfloat16)


def steps_of(stream_key, dims, pieces, smallest, high):
    def one(position, shards_of):
        steps = jax.random.uniform(jax.random.fold_in(jax.random.fold_in(stream_key, 6), position), (shards_of,), jnp.float32, smallest / len(pieces), high / len(pieces))
        return jnp.repeat(jnp.exp(steps), dims[position] // shards_of).reshape((-1,) + (1,) * (len(dims) - position - 1))

    loudness = one(*pieces[0])
    for cut in pieces[1:]:
        loudness = loudness * one(*cut)
    return loudness


def normal_values(rng, dims, deviation, bound, shards=(), kind=jnp.bfloat16):
    drawn = jax.random.normal(rng, dims, jnp.float32) * deviation
    if len(shards) > 0:
        drawn = steps_of(rng, dims, shards, -0.22, 0.18) * drawn
    return jnp.clip(drawn, min=-bound, max=bound).astype(kind)


def setup_inputs(seed: int = 0) -> dict:
    seeds = jax.random.split(jax.random.key(seed), 5)
    return {
        "inputs": draw_inputs(jax.random.fold_in(seeds[4], 71), 0),
        "down_weight": draw_down_weight(jax.random.fold_in(seeds[4], 71), 0),
        "up_weight": normal_values(seeds[2], (SEGMENTS, L, FEAT), L ** -0.5, 0.25, ((0, 4), (1, 4), (2, 2))),
        "value_grad": normal_values(seeds[3], (SEGMENTS, TOKENS, FEAT), 0.2, 1.1953125, ((0, 4), (1, 4), (2, 2))),
    }


def block_sum(left, right):
    left_blocks = left.reshape(N_ROW, TOK_ROW, left.shape[1]).astype(jnp.float32)
    right_blocks = right.reshape(N_ROW, TOK_ROW, right.shape[1]).astype(jnp.float32)
    terms = jnp.einsum('btl,btf->blf', left_blocks, right_blocks)
    rounded = lax.optimization_barrier(terms.astype(jnp.bfloat16))
    return lax.optimization_barrier(jnp.sum(rounded.astype(jnp.float32), axis=0)).astype(jnp.bfloat16)

def segment_grads(operands):
    inputs, down_weight, up_weight, value_grad = operands
    latent = jnp.dot(inputs, down_weight.T, preferred_element_type=jnp.float32)
    inv_rms = lax.rsqrt(lax.optimization_barrier(jnp.mean(latent * latent, axis=-1, keepdims=True)) + 1e-06)
    normed = latent * inv_rms
    normed_bf = normed.astype(jnp.bfloat16)
    normed_grad = jnp.dot(value_grad, up_weight.T, preferred_element_type=jnp.float32)
    up_grad = block_sum(normed_bf, value_grad)
    inner = lax.optimization_barrier(jnp.mean(normed_grad * normed, axis=-1, keepdims=True))
    latent_grad = inv_rms * (normed_grad - normed * inner)
    latent_bf = latent_grad.astype(jnp.bfloat16)
    down_grad = block_sum(latent_bf, inputs)
    input_grad = jnp.dot(latent_bf, down_weight, preferred_element_type=jnp.float32).astype(jnp.bfloat16)
    return (input_grad, down_grad, up_grad)

def reference(inputs, down_weight, up_weight, value_grad):
    input_grad, down_grad, up_grad = lax.map(segment_grads, (inputs, down_weight, up_weight, value_grad))
    filler = jnp.zeros((1, TOKENS, D), jnp.bfloat16)
    passed_grad = jnp.concatenate([input_grad[1:], filler], axis=0)
    return (passed_grad, down_grad, up_grad)
```

```python
import jax
import jax.numpy as jnp
from jax import lax
from jax.sharding import PartitionSpec as P

F32 = jnp.float32
BF16 = jnp.bfloat16
SLICES = 4


def shifted(value, axis, steps):
    count = lax.axis_size(axis)
    leading, last = (max(0, -steps), min(count, count - steps))
    return lax.ppermute(value, axis, [(source, source + steps) for source in range(leading, last)])


def general_body(inputs, down_weight, up_weight, value_grad):
    tokens = inputs[0]
    cotangent = value_grad[0]
    down_full = lax.all_gather(down_weight[0], "row", axis=0, tiled=True)
    up_full = lax.all_gather(up_weight[0], "row", axis=0, tiled=True)
    latent_part = jnp.einsum("td,ld->tl", tokens, down_full, preferred_element_type=F32)
    grad_part = jnp.einsum("tf,lf->tl", cotangent, up_full, preferred_element_type=F32)
    latent = lax.psum(latent_part.astype(BF16), "col").astype(F32)
    normed_grad = lax.psum(grad_part.astype(BF16), "col").astype(F32)
    inv_rms = lax.rsqrt(jnp.mean(latent * latent, axis=-1, keepdims=True) + 1e-06)
    normed = latent * inv_rms
    normed_bf = normed.astype(BF16)
    inner = jnp.mean(normed_grad * normed, axis=-1, keepdims=True)
    latent_bf = (inv_rms * (normed_grad - normed * inner)).astype(BF16)
    up_grad = lax.psum_scatter(
        jnp.einsum("tl,tf->lf", normed_bf, cotangent, preferred_element_type=F32).astype(BF16),
        "row",
        scatter_dimension=0,
        tiled=True,
    )
    down_grad = lax.psum_scatter(
        jnp.einsum("tl,td->ld", latent_bf, tokens, preferred_element_type=F32).astype(BF16),
        "row",
        scatter_dimension=0,
        tiled=True,
    )
    input_grad = jnp.einsum("tl,ld->td", latent_bf, down_full, preferred_element_type=F32)
    passed = shifted(input_grad.astype(BF16), "section", -1)
    return (passed[None], down_grad[None], up_grad[None])


def inward(value):
    return lax.ppermute(value, "row", [(0, 1), (3, 2)])


def across(value):
    return lax.ppermute(value, "row", [(1, 2), (2, 1)])


def outward(value):
    return lax.ppermute(value, "row", [(1, 0), (2, 3)])


def other_col(value):
    return lax.ppermute(value, "col", [(0, 1), (1, 0)])


def rows_dot(left, right):
    return lax.dot_general(left, right, (((1,), (1,)), ((), ())), preferred_element_type=F32)


def tokens_dot(left, right):
    return lax.dot_general(left, right, (((0,), (0,)), ((), ())), preferred_element_type=F32)


def col_sum(part):
    sent = part.astype(BF16)
    return sent.astype(F32) + other_col(sent).astype(F32)


def folded_body(inputs, down_weight, up_weight, value_grad):
    tokens, down, up, cotangent = inputs[0], down_weight[0], up_weight[0], value_grad[0]
    rows, width = tokens.shape
    lat = down.shape[0]
    feat = cotangent.shape[1]
    sections = lax.axis_size("section")
    place = lax.axis_index("row")
    middle = (place == 1) | (place == 2)

    down_end = inward(down)
    tokens_end = inward(tokens)
    down_other = across(down)
    down_other_end = across(down_end)

    pieces = []
    step = feat // SLICES
    for k in range(SLICES):
        cut = slice(k * step, (k + 1) * step)
        own = cotangent[:, cut]
        moved = inward(jnp.concatenate([own, up[:, cut]], axis=0))
        other = across(own)
        other_end = across(moved[:rows])
        pieces.append((
            jnp.concatenate([own, moved[:rows], other, other_end], axis=0),
            jnp.concatenate([up[:, cut], moved[rows:]], axis=0),
        ))

    tokens_mine = jnp.concatenate([tokens, tokens_end], axis=0)
    down_all = jnp.concatenate([down, down_end, down_other, down_other_end], axis=0)
    latent = col_sum(rows_dot(tokens_mine, down_all))
    inv_rms = lax.rsqrt(jnp.mean(latent * latent, axis=-1, keepdims=True) + 1e-06)
    normed = latent * inv_rms
    normed_bf = normed.astype(BF16)
    normed_all = jnp.concatenate(
        [normed_bf[:, : 2 * lat], across(normed_bf[:, 2 * lat :])], axis=0
    )

    grad_part = None
    up_pieces = []
    for values, weights in pieces:
        term = rows_dot(values, weights)
        grad_part = term if grad_part is None else grad_part + term
        up_piece = tokens_dot(normed_all, values).astype(BF16)
        back = outward(up_piece[lat:])
        up_pieces.append(jnp.where(middle, up_piece[:lat], back))
    up_grad = jnp.concatenate(up_pieces, axis=1)

    grad_mine = col_sum(grad_part[: 2 * rows])
    grad_other = col_sum(grad_part[2 * rows :])
    normed_grad = jnp.concatenate([grad_mine, across(grad_other.astype(BF16)).astype(F32)], axis=1)
    inner = jnp.mean(normed_grad * normed, axis=-1, keepdims=True)
    latent_bf = (inv_rms * (normed_grad - normed * inner)).astype(BF16)

    sums = [
        tokens_dot(latent_bf[:, j * lat : (j + 1) * lat], tokens_mine) for j in range(4)
    ]
    from_end = across(sums[3].astype(BF16))
    from_own = across(sums[2].astype(BF16))
    down_end_grad = outward((sums[1] + from_end.astype(F32)).astype(BF16))
    down_own_grad = (sums[0] + from_own.astype(F32)).astype(BF16)
    down_grad = jnp.where(middle, down_own_grad, down_end_grad)

    input_grad = jnp.dot(latent_bf, down_all, preferred_element_type=F32).astype(BF16)
    passed_own = shifted(input_grad[:rows], "section", -1)
    passed_end = lax.ppermute(
        input_grad[rows:],
        ("section", "row"),
        [
            (4 * s + source, 4 * (s - 1) + target)
            for s in range(1, sections)
            for source, target in ((1, 0), (2, 3))
        ],
    )
    passed = jnp.where(middle, passed_own, passed_end)
    return (passed[None], down_grad[None], up_grad[None])


def solution(mesh):
    spec = P("section", "row", "col")
    folds = mesh.shape["row"] == 4 and mesh.shape["col"] == 2
    return jax.shard_map(
        folded_body if folds else general_body,
        mesh=mesh,
        in_specs=(spec,) * 4,
        out_specs=(spec,) * 3,
        check_vma=False,
    )
```

```python
import jax
import jax.numpy as jnp
from jax import lax
from jax.sharding import PartitionSpec as P

F32 = jnp.float32
BF16 = jnp.bfloat16


def shifted(value, axis, steps):
    count = lax.axis_size(axis)
    leading, last = (max(0, -steps), min(count, count - steps))
    return lax.ppermute(value, axis, [(source, source + steps) for source in range(leading, last)])


def general_body(inputs, down_weight, up_weight, value_grad):
    tokens = inputs[0]
    cotangent = value_grad[0]
    down_full = lax.all_gather(down_weight[0], "row", axis=0, tiled=True)
    up_full = lax.all_gather(up_weight[0], "row", axis=0, tiled=True)
    latent_part = jnp.einsum("td,ld->tl", tokens, down_full, preferred_element_type=F32)
    grad_part = jnp.einsum("tf,lf->tl", cotangent, up_full, preferred_element_type=F32)
    latent = lax.psum(latent_part.astype(BF16), "col").astype(F32)
    normed_grad = lax.psum(grad_part.astype(BF16), "col").astype(F32)
    inv_rms = lax.rsqrt(jnp.mean(latent * latent, axis=-1, keepdims=True) + 1e-06)
    normed = latent * inv_rms
    normed_bf = normed.astype(BF16)
    inner = jnp.mean(normed_grad * normed, axis=-1, keepdims=True)
    latent_bf = (inv_rms * (normed_grad - normed * inner)).astype(BF16)
    up_grad = lax.psum_scatter(
        jnp.einsum("tl,tf->lf", normed_bf, cotangent, preferred_element_type=F32).astype(BF16),
        "row",
        scatter_dimension=0,
        tiled=True,
    )
    down_grad = lax.psum_scatter(
        jnp.einsum("tl,td->ld", latent_bf, tokens, preferred_element_type=F32).astype(BF16),
        "row",
        scatter_dimension=0,
        tiled=True,
    )
    input_grad = jnp.einsum("tl,ld->td", latent_bf, down_full, preferred_element_type=F32)
    passed = shifted(input_grad.astype(BF16), "section", -1)
    return (passed[None], down_grad[None], up_grad[None])


def inward(value):
    return lax.ppermute(value, "row", [(0, 1), (3, 2)])


def across(value):
    return lax.ppermute(value, "row", [(1, 2), (2, 1)])


def outward(value):
    return lax.ppermute(value, "row", [(1, 0), (2, 3)])


def other_col(value):
    return lax.ppermute(value, "col", [(0, 1), (1, 0)])


def after(value, *earlier):
    return lax.optimization_barrier((value, *earlier))[0]


def rows_dot(left, right):
    return lax.dot_general(left, right, (((1,), (1,)), ((), ())), preferred_element_type=F32)


def tokens_dot(left, right):
    return lax.dot_general(left, right, (((0,), (0,)), ((), ())), preferred_element_type=F32)


def col_sum(part):
    sent = part.astype(BF16)
    return sent.astype(F32) + other_col(sent).astype(F32)


def folded_body(inputs, down_weight, up_weight, value_grad):
    tokens, down, up, cotangent = inputs[0], down_weight[0], up_weight[0], value_grad[0]
    rows, width = tokens.shape
    lat = down.shape[0]
    feat = cotangent.shape[1]
    sections = lax.axis_size("section")
    place = lax.axis_index("row")
    middle = (place == 1) | (place == 2)

    half = feat // 2
    cuts = (slice(0, half), slice(half, feat))
    cot_other = [across(cotangent[:, cut]) for cut in cuts]
    down_other = across(down)
    down_end = inward(down)
    tokens_end = inward(tokens)
    first = after(cotangent[:, cuts[0]], down_end, cot_other[0])
    second = after(cotangent[:, cuts[1]], tokens_end, cot_other[1])
    cot_end = (inward(first), inward(second))
    up_end = inward(after(up, cot_end[0]))
    down_other_end = across(down_end)
    cot_other_end_first = across(cot_end[0])

    tokens_mine = jnp.concatenate([tokens, tokens_end], axis=0)
    down_all = jnp.concatenate([down, down_end, down_other, down_other_end], axis=0)
    latent = col_sum(rows_dot(tokens_mine, down_all))
    inv_rms = lax.rsqrt(jnp.mean(latent * latent, axis=-1, keepdims=True) + 1e-06)
    normed = latent * inv_rms
    normed_bf = normed.astype(BF16)
    normed_sent = normed_bf[:, 2 * lat :]
    normed_other = across(normed_sent)
    normed_all = jnp.concatenate([normed_bf[:, : 2 * lat], normed_other], axis=0)

    cot_other_end = (cot_other_end_first, across(after(cot_end[1], normed_sent)))
    up_mine = jnp.concatenate([up, up_end], axis=0)
    grad_part = None
    up_local, up_back = [], []
    for k, cut in enumerate(cuts):
        values = jnp.concatenate(
            [cotangent[:, cut], cot_end[k], cot_other[k], cot_other_end[k]], axis=0
        )
        up_piece = tokens_dot(normed_all, values).astype(BF16)
        up_local.append(up_piece)
        up_back.append(outward(up_piece[lat:]))
        term = rows_dot(values, up_mine[:, cut])
        grad_part = term if grad_part is None else grad_part + term
    up_grad = jnp.concatenate(
        [jnp.where(middle, piece[:lat], back) for piece, back in zip(up_local, up_back)], axis=1
    )

    grad_other = col_sum(grad_part[2 * rows :])
    grad_mine = col_sum(grad_part[: 2 * rows])
    normed_grad = jnp.concatenate([grad_mine, across(grad_other.astype(BF16)).astype(F32)], axis=1)
    inner = jnp.mean(normed_grad * normed, axis=-1, keepdims=True)
    latent_bf = (inv_rms * (normed_grad - normed * inner)).astype(BF16)
    latent_bf = after(latent_bf, *up_local)

    sums = [
        tokens_dot(latent_bf[:, j * lat : (j + 1) * lat], tokens_mine) for j in range(4)
    ]
    sent_end, sent_own = sums[3].astype(BF16), sums[2].astype(BF16)
    from_end, from_own = across(sent_end), across(sent_own)
    down_end_grad = outward((sums[1] + from_end.astype(F32)).astype(BF16))
    down_own_grad = (sums[0] + from_own.astype(F32)).astype(BF16)
    down_grad = jnp.where(middle, down_own_grad, down_end_grad)

    latent_bf = after(latent_bf, sent_end, sent_own)
    input_grad = jnp.dot(latent_bf, down_all, preferred_element_type=F32).astype(BF16)
    passed_own = shifted(input_grad[:rows], "section", -1)
    passed_end = lax.ppermute(
        input_grad[rows:],
        ("section", "row"),
        [
            (4 * s + source, 4 * (s - 1) + target)
            for s in range(1, sections)
            for source, target in ((1, 0), (2, 3))
        ],
    )
    passed = jnp.where(middle, passed_own, passed_end)
    return (passed[None], down_grad[None], up_grad[None])


def solution(mesh):
    spec = P("section", "row", "col")
    folds = mesh.shape["row"] == 4 and mesh.shape["col"] == 2
    return jax.shard_map(
        folded_body if folds else general_body,
        mesh=mesh,
        in_specs=(spec,) * 4,
        out_specs=(spec,) * 3,
        check_vma=False,
    )
```

```python
import jax
import jax.numpy as jnp
from jax import lax
from jax.sharding import PartitionSpec as P

F32 = jnp.float32
BF16 = jnp.bfloat16


def shifted(value, axis, steps):
    count = lax.axis_size(axis)
    leading, last = (max(0, -steps), min(count, count - steps))
    return lax.ppermute(value, axis, [(source, source + steps) for source in range(leading, last)])


def general_body(inputs, down_weight, up_weight, value_grad):
    tokens = inputs[0]
    cotangent = value_grad[0]
    down_full = lax.all_gather(down_weight[0], "row", axis=0, tiled=True)
    up_full = lax.all_gather(up_weight[0], "row", axis=0, tiled=True)
    latent_part = jnp.einsum("td,ld->tl", tokens, down_full, preferred_element_type=F32)
    grad_part = jnp.einsum("tf,lf->tl", cotangent, up_full, preferred_element_type=F32)
    latent = lax.psum(latent_part.astype(BF16), "col").astype(F32)
    normed_grad = lax.psum(grad_part.astype(BF16), "col").astype(F32)
    inv_rms = lax.rsqrt(jnp.mean(latent * latent, axis=-1, keepdims=True) + 1e-06)
    normed = latent * inv_rms
    normed_bf = normed.astype(BF16)
    inner = jnp.mean(normed_grad * normed, axis=-1, keepdims=True)
    latent_bf = (inv_rms * (normed_grad - normed * inner)).astype(BF16)
    up_grad = lax.psum_scatter(
        jnp.einsum("tl,tf->lf", normed_bf, cotangent, preferred_element_type=F32).astype(BF16),
        "row",
        scatter_dimension=0,
        tiled=True,
    )
    down_grad = lax.psum_scatter(
        jnp.einsum("tl,td->ld", latent_bf, tokens, preferred_element_type=F32).astype(BF16),
        "row",
        scatter_dimension=0,
        tiled=True,
    )
    input_grad = jnp.einsum("tl,ld->td", latent_bf, down_full, preferred_element_type=F32)
    passed = shifted(input_grad.astype(BF16), "section", -1)
    return (passed[None], down_grad[None], up_grad[None])


def inward(value):
    return lax.ppermute(value, "row", [(0, 1), (3, 2)])


def across(value):
    return lax.ppermute(value, "row", [(1, 2), (2, 1)])


def outward(value):
    return lax.ppermute(value, "row", [(1, 0), (2, 3)])


def other_col(value):
    return lax.ppermute(value, "col", [(0, 1), (1, 0)])


def after(value, *earlier):
    return lax.optimization_barrier((value, *earlier))[0]


def rows_dot(left, right):
    return lax.dot_general(left, right, (((1,), (1,)), ((), ())), preferred_element_type=F32)


def tokens_dot(left, right):
    return lax.dot_general(left, right, (((0,), (0,)), ((), ())), preferred_element_type=F32)


def col_sum(part):
    sent = part.astype(BF16)
    return sent.astype(F32) + other_col(sent).astype(F32)


def folded_body(inputs, down_weight, up_weight, value_grad):
    tokens, down, up, cotangent = inputs[0], down_weight[0], up_weight[0], value_grad[0]
    rows, width = tokens.shape
    lat = down.shape[0]
    feat = cotangent.shape[1]
    sections = lax.axis_size("section")
    place = lax.axis_index("row")
    middle = (place == 1) | (place == 2)

    half = feat // 2
    cuts = (slice(0, half), slice(half, feat))
    cot_own = [cotangent[:, cut] for cut in cuts]
    down_end = inward(down)
    down_other = across(down)
    cot_end_first = inward(cot_own[0])
    cot_other = across(cotangent)
    tokens_end = inward(tokens)
    down_other_end = across(down_end)
    cot_other_end_first = across(cot_end_first)
    cot_end_second = inward(after(cot_own[1], down_end, down_other))
    up_end = inward(after(up, tokens_end, cot_end_first))

    tokens_mine = jnp.concatenate([tokens, tokens_end], axis=0)
    down_all = jnp.concatenate([down, down_end, down_other, down_other_end], axis=0)
    latent = col_sum(rows_dot(tokens_mine, down_all))
    inv_rms = lax.rsqrt(jnp.mean(latent * latent, axis=-1, keepdims=True) + 1e-06)
    normed = latent * inv_rms
    normed_bf = normed.astype(BF16)
    normed_sent = normed_bf[:, 2 * lat :]
    normed_other = across(normed_sent)
    normed_all = jnp.concatenate([normed_bf[:, : 2 * lat], normed_other], axis=0)

    cot_end = (cot_end_first, cot_end_second)
    cot_other_end = (cot_other_end_first, across(after(cot_end_second, normed_sent)))

    up_local, up_back = [], []
    for k, cut in enumerate(cuts):
        values = jnp.concatenate(
            [cotangent[:, cut], cot_end[k], cot_other[:, cut], cot_other_end[k]], axis=0
        )
        up_piece = tokens_dot(normed_all, values).astype(BF16)
        up_local.append(up_piece)
        up_back.append(outward(up_piece[lat:]))
    up_grad = jnp.concatenate(
        [jnp.where(middle, piece[:lat], back) for piece, back in zip(up_local, up_back)], axis=1
    )

    up_mine = jnp.concatenate([up, after(up_end, up_local[0])], axis=0)
    early = rows_dot(jnp.concatenate([cotangent, cot_other], axis=0), up_mine)
    early_end = sum(rows_dot(cot_end[k], up_mine[:, cut]) for k, cut in enumerate(cuts))
    late = sum(rows_dot(cot_other_end[k], up_mine[:, cut]) for k, cut in enumerate(cuts))
    early = col_sum(jnp.concatenate([early, early_end], axis=0))
    late = col_sum(late)

    def latent_grad(which, mine, other):
        normed_grad = jnp.concatenate([mine, other.astype(F32)], axis=1)
        inner = jnp.mean(normed_grad * normed[which], axis=-1, keepdims=True)
        return (inv_rms[which] * (normed_grad - normed[which] * inner)).astype(BF16)

    own_rows, end_rows = slice(0, rows), slice(rows, 2 * rows)
    grad_own = across(early[rows : 2 * rows].astype(BF16))
    grad_end = across(late.astype(BF16))
    latent_own = latent_grad(own_rows, early[:rows], grad_own)
    latent_end = latent_grad(end_rows, early[2 * rows :], grad_end)
    latent_bf = jnp.concatenate([latent_own, latent_end], axis=0)
    sums = [
        tokens_dot(latent_bf[:, j * lat : (j + 1) * lat], tokens_mine) for j in range(4)
    ]
    sent_end, sent_own = sums[3].astype(BF16), sums[2].astype(BF16)
    from_end, from_own = across(sent_end), across(sent_own)
    down_end_grad = outward((sums[1] + from_end.astype(F32)).astype(BF16))
    down_own_grad = (sums[0] + from_own.astype(F32)).astype(BF16)
    down_grad = jnp.where(middle, down_own_grad, down_end_grad)

    latent_bf = after(latent_bf, sent_end, sent_own)
    input_grad = jnp.dot(latent_bf, down_all, preferred_element_type=F32).astype(BF16)
    passed_end = lax.ppermute(
        input_grad[rows:],
        ("section", "row"),
        [
            (4 * s + source, 4 * (s - 1) + target)
            for s in range(1, sections)
            for source, target in ((1, 0), (2, 3))
        ],
    )
    passed_own = shifted(after(input_grad[:rows], from_end), "section", -1)
    passed = jnp.where(middle, passed_own, passed_end)
    return (passed[None], down_grad[None], up_grad[None])


def solution(mesh):
    spec = P("section", "row", "col")
    folds = mesh.shape["row"] == 4 and mesh.shape["col"] == 2
    return jax.shard_map(
        folded_body if folds else general_body,
        mesh=mesh,
        in_specs=(spec,) * 4,
        out_specs=(spec,) * 3,
        check_vma=False,
    )
```

```python
import jax
import jax.numpy as jnp
from jax import lax
from jax.sharding import PartitionSpec as P

F32 = jnp.float32
BF16 = jnp.bfloat16


def shifted(value, axis, steps):
    count = lax.axis_size(axis)
    leading, last = (max(0, -steps), min(count, count - steps))
    return lax.ppermute(value, axis, [(source, source + steps) for source in range(leading, last)])


def general_body(inputs, down_weight, up_weight, value_grad):
    tokens = inputs[0]
    cotangent = value_grad[0]
    down_full = lax.all_gather(down_weight[0], "row", axis=0, tiled=True)
    up_full = lax.all_gather(up_weight[0], "row", axis=0, tiled=True)
    latent_part = jnp.einsum("td,ld->tl", tokens, down_full, preferred_element_type=F32)
    grad_part = jnp.einsum("tf,lf->tl", cotangent, up_full, preferred_element_type=F32)
    latent = lax.psum(latent_part.astype(BF16), "col").astype(F32)
    normed_grad = lax.psum(grad_part.astype(BF16), "col").astype(F32)
    inv_rms = lax.rsqrt(jnp.mean(latent * latent, axis=-1, keepdims=True) + 1e-06)
    normed = latent * inv_rms
    normed_bf = normed.astype(BF16)
    inner = jnp.mean(normed_grad * normed, axis=-1, keepdims=True)
    latent_bf = (inv_rms * (normed_grad - normed * inner)).astype(BF16)
    up_grad = lax.psum_scatter(
        jnp.einsum("tl,tf->lf", normed_bf, cotangent, preferred_element_type=F32).astype(BF16),
        "row",
        scatter_dimension=0,
        tiled=True,
    )
    down_grad = lax.psum_scatter(
        jnp.einsum("tl,td->ld", latent_bf, tokens, preferred_element_type=F32).astype(BF16),
        "row",
        scatter_dimension=0,
        tiled=True,
    )
    input_grad = jnp.einsum("tl,ld->td", latent_bf, down_full, preferred_element_type=F32)
    passed = shifted(input_grad.astype(BF16), "section", -1)
    return (passed[None], down_grad[None], up_grad[None])


def inward(value):
    return lax.ppermute(value, "row", [(0, 1), (3, 2)])


def across(value):
    return lax.ppermute(value, "row", [(1, 2), (2, 1)])


def outward(value):
    return lax.ppermute(value, "row", [(1, 0), (2, 3)])


def other_col(value):
    return lax.ppermute(value, "col", [(0, 1), (1, 0)])


def after(value, *earlier):
    return lax.optimization_barrier((value, *earlier))[0]


def rows_dot(left, right):
    return lax.dot_general(left, right, (((1,), (1,)), ((), ())), preferred_element_type=F32)


def tokens_dot(left, right):
    return lax.dot_general(left, right, (((0,), (0,)), ((), ())), preferred_element_type=F32)


def col_sum(part):
    sent = part.astype(BF16)
    return sent.astype(F32) + other_col(sent).astype(F32)


def folded_body(inputs, down_weight, up_weight, value_grad):
    tokens, down, up, cotangent = inputs[0], down_weight[0], up_weight[0], value_grad[0]
    rows, width = tokens.shape
    lat = down.shape[0]
    feat = cotangent.shape[1]
    sections = lax.axis_size("section")
    place = lax.axis_index("row")
    middle = (place == 1) | (place == 2)

    half = feat // 2
    cuts = (slice(0, half), slice(half, feat))
    cot_own = [cotangent[:, cut] for cut in cuts]
    down_end = inward(down)
    down_other = across(down)
    cot_end_first = inward(cot_own[0])
    cot_other = across(cotangent)
    tokens_end = inward(tokens)
    down_other_end = across(down_end)
    cot_other_end_first = across(cot_end_first)
    cot_end_second = inward(after(cot_own[1], down_end, down_other))
    up_end = inward(after(up, cot_other, cot_end_first))

    tokens_mine = jnp.concatenate([tokens, tokens_end], axis=0)
    down_all = jnp.concatenate([down, down_end, down_other, down_other_end], axis=0)
    latent = col_sum(rows_dot(tokens_mine, down_all))
    inv_rms = lax.rsqrt(jnp.mean(latent * latent, axis=-1, keepdims=True) + 1e-06)
    normed = latent * inv_rms
    normed_bf = normed.astype(BF16)
    normed_sent = normed_bf[:, 2 * lat :]
    normed_other = across(normed_sent)
    normed_all = jnp.concatenate([normed_bf[:, : 2 * lat], normed_other], axis=0)

    cot_end = (cot_end_first, cot_end_second)
    cot_other_end_second = across(after(cot_end_second, normed_sent))

    def up_product(k, other_end):
        values = [cotangent[:, cuts[k]], cot_end[k], cot_other[:, cuts[k]], other_end]
        return tokens_dot(normed_all, jnp.concatenate(values, axis=0)).astype(BF16)

    up_first = up_product(0, cot_other_end_first)
    up_back_first = outward(up_first[lat:])

    up_mine = jnp.concatenate([up, after(up_end, up_first)], axis=0)
    early = rows_dot(jnp.concatenate([cotangent, cot_other], axis=0), up_mine)
    early_end = sum(rows_dot(cot_end[k], up_mine[:, cut]) for k, cut in enumerate(cuts))
    late_first = rows_dot(cot_other_end_first, up_mine[:, cuts[0]])
    early = after(jnp.concatenate([early, early_end], axis=0).astype(BF16), late_first)
    early = early.astype(F32) + other_col(early).astype(F32)

    last, _ = lax.optimization_barrier((cot_other_end_second, early))
    late = col_sum(late_first + rows_dot(last, up_mine[:, cuts[1]]))
    up_second = up_product(1, last)
    up_back_second = outward(up_second[lat:])
    up_grad = jnp.concatenate(
        [
            jnp.where(middle, up_first[:lat], up_back_first),
            jnp.where(middle, up_second[:lat], up_back_second),
        ],
        axis=1,
    )

    def latent_grad(which, mine, other):
        normed_grad = jnp.concatenate([mine, other.astype(F32)], axis=1)
        inner = jnp.mean(normed_grad * normed[which], axis=-1, keepdims=True)
        return (inv_rms[which] * (normed_grad - normed[which] * inner)).astype(BF16)

    own_rows, end_rows = slice(0, rows), slice(rows, 2 * rows)
    grad_own = across(early[rows : 2 * rows].astype(BF16))
    grad_end = across(after(late.astype(BF16), up_second))
    latent_own = latent_grad(own_rows, early[:rows], grad_own)
    latent_end = latent_grad(end_rows, early[2 * rows :], grad_end)
    input_end = jnp.dot(latent_end, down_all, preferred_element_type=F32).astype(BF16)
    passed_end = lax.ppermute(
        input_end,
        ("section", "row"),
        [
            (4 * s + source, 4 * (s - 1) + target)
            for s in range(1, sections)
            for source, target in ((1, 0), (2, 3))
        ],
    )

    latent_bf = after(jnp.concatenate([latent_own, latent_end], axis=0), input_end)
    sums = [
        tokens_dot(latent_bf[:, j * lat : (j + 1) * lat], tokens_mine) for j in range(4)
    ]
    sent_end, sent_own = sums[3].astype(BF16), sums[2].astype(BF16)
    from_end, from_own = across(sent_end), across(after(sent_own, up_back_second))
    down_end_grad = outward((sums[1] + from_end.astype(F32)).astype(BF16))
    down_own_grad = (sums[0] + from_own.astype(F32)).astype(BF16)
    down_grad = jnp.where(middle, down_own_grad, down_end_grad)

    latent_own = after(latent_own, sent_end, sent_own)
    input_own = jnp.dot(latent_own, down_all, preferred_element_type=F32).astype(BF16)
    passed_own = shifted(after(input_own, from_end, passed_end), "section", -1)
    passed = jnp.where(middle, passed_own, passed_end)
    return (passed[None], down_grad[None], up_grad[None])


def solution(mesh):
    spec = P("section", "row", "col")
    folds = mesh.shape["row"] == 4 and mesh.shape["col"] == 2
    return jax.shard_map(
        folded_body if folds else general_body,
        mesh=mesh,
        in_specs=(spec,) * 4,
        out_specs=(spec,) * 3,
        check_vma=False,
    )
```

```python
import jax
import jax.numpy as jnp
from jax import lax
from jax.sharding import PartitionSpec as P

F32 = jnp.float32
BF16 = jnp.bfloat16


def shifted(value, axis, steps):
    count = lax.axis_size(axis)
    leading, last = (max(0, -steps), min(count, count - steps))
    return lax.ppermute(value, axis, [(source, source + steps) for source in range(leading, last)])


def general_body(inputs, down_weight, up_weight, value_grad):
    tokens = inputs[0]
    cotangent = value_grad[0]
    down_full = lax.all_gather(down_weight[0], "row", axis=0, tiled=True)
    up_full = lax.all_gather(up_weight[0], "row", axis=0, tiled=True)
    latent_part = jnp.einsum("td,ld->tl", tokens, down_full, preferred_element_type=F32)
    grad_part = jnp.einsum("tf,lf->tl", cotangent, up_full, preferred_element_type=F32)
    latent = lax.psum(latent_part.astype(BF16), "col").astype(F32)
    normed_grad = lax.psum(grad_part.astype(BF16), "col").astype(F32)
    inv_rms = lax.rsqrt(jnp.mean(latent * latent, axis=-1, keepdims=True) + 1e-06)
    normed = latent * inv_rms
    normed_bf = normed.astype(BF16)
    inner = jnp.mean(normed_grad * normed, axis=-1, keepdims=True)
    latent_bf = (inv_rms * (normed_grad - normed * inner)).astype(BF16)
    up_grad = lax.psum_scatter(
        jnp.einsum("tl,tf->lf", normed_bf, cotangent, preferred_element_type=F32).astype(BF16),
        "row",
        scatter_dimension=0,
        tiled=True,
    )
    down_grad = lax.psum_scatter(
        jnp.einsum("tl,td->ld", latent_bf, tokens, preferred_element_type=F32).astype(BF16),
        "row",
        scatter_dimension=0,
        tiled=True,
    )
    input_grad = jnp.einsum("tl,ld->td", latent_bf, down_full, preferred_element_type=F32)
    passed = shifted(input_grad.astype(BF16), "section", -1)
    return (passed[None], down_grad[None], up_grad[None])


def inward(value):
    return lax.ppermute(value, "row", [(0, 1), (3, 2)])


def across(value):
    return lax.ppermute(value, "row", [(1, 2), (2, 1)])


def outward(value):
    return lax.ppermute(value, "row", [(1, 0), (2, 3)])


def other_col(value):
    return lax.ppermute(value, "col", [(0, 1), (1, 0)])


def after(value, *earlier):
    return lax.optimization_barrier((value, *earlier))[0]


def rows_dot(left, right):
    return lax.dot_general(left, right, (((1,), (1,)), ((), ())), preferred_element_type=F32)


def tokens_dot(left, right):
    return lax.dot_general(left, right, (((0,), (0,)), ((), ())), preferred_element_type=F32)


def col_sum(part):
    sent = part.astype(BF16)
    return sent.astype(F32) + other_col(sent).astype(F32)


def folded_body(inputs, down_weight, up_weight, value_grad):
    tokens, down, up, cotangent = inputs[0], down_weight[0], up_weight[0], value_grad[0]
    rows, width = tokens.shape
    lat = down.shape[0]
    feat = cotangent.shape[1]
    sections = lax.axis_size("section")
    place = lax.axis_index("row")
    middle = (place == 1) | (place == 2)

    cut = feat * 5 // 8 // 128 * 128
    cuts = (slice(0, cut), slice(cut, feat))
    cot_own = [cotangent[:, c] for c in cuts]
    down_end = inward(down)
    tokens_end = inward(tokens)
    cot_other = [across(cot_own[0])]
    down_other = across(down)
    cot_end = [inward(after(cot_own[0], down_end, cot_other[0]))]
    down_other_end = across(down_end)
    cot_other.append(across(cot_own[1]))
    cot_end.append(inward(after(cot_own[1], tokens_end, down_other)))
    cot_other_end = [across(cot_end[0])]
    up_end = inward(after(up, cot_end[0], cot_other[1]))

    tokens_mine = jnp.concatenate([tokens, tokens_end], axis=0)
    down_all = jnp.concatenate([down, down_end, down_other, down_other_end], axis=0)
    latent = col_sum(rows_dot(tokens_mine, down_all))
    inv_rms = lax.rsqrt(jnp.mean(latent * latent, axis=-1, keepdims=True) + 1e-06)
    normed = latent * inv_rms
    normed_bf = normed.astype(BF16)
    normed_sent = normed_bf[:, 2 * lat :]
    normed_other = across(normed_sent)
    normed_all = jnp.concatenate([normed_bf[:, : 2 * lat], normed_other], axis=0)

    cot_other_end.append(across(after(cot_end[1], normed_sent)))
    cot_all = [
        jnp.concatenate([cot_own[k], cot_end[k], cot_other[k], cot_other_end[k]], axis=0)
        for k in range(2)
    ]

    up_first = tokens_dot(normed_all, cot_all[0]).astype(BF16)
    back_first = outward(up_first[lat:])
    up_mine = jnp.concatenate([up, after(up_end, up_first)], axis=0)
    grad = rows_dot(cot_all[0], up_mine[:, cuts[0]]) + rows_dot(cot_all[1], up_mine[:, cuts[1]])
    grad_other = col_sum(grad[2 * rows :])
    grad_mine = col_sum(grad[: 2 * rows])
    up_second = tokens_dot(normed_all, cot_all[1]).astype(BF16)
    back_second = outward(up_second[lat:])
    up_grad = jnp.concatenate(
        [
            jnp.where(middle, up_first[:lat], back_first),
            jnp.where(middle, up_second[:lat], back_second),
        ],
        axis=1,
    )

    grad_sent = after(grad_other.astype(BF16), up_second, back_first)
    normed_grad = jnp.concatenate([grad_mine, across(grad_sent).astype(F32)], axis=1)
    inner = jnp.mean(normed_grad * normed, axis=-1, keepdims=True)
    latent_bf = (inv_rms * (normed_grad - normed * inner)).astype(BF16)
    input_end = jnp.dot(latent_bf[rows:], down_all, preferred_element_type=F32).astype(BF16)
    passed_end = lax.ppermute(
        input_end,
        ("section", "row"),
        [
            (4 * s + source, 4 * (s - 1) + target)
            for s in range(1, sections)
            for source, target in ((1, 0), (2, 3))
        ],
    )

    latent_bf = after(latent_bf, input_end)
    sums = [
        tokens_dot(latent_bf[:, j * lat : (j + 1) * lat], tokens_mine) for j in range(4)
    ]
    sent_end, sent_own = sums[3].astype(BF16), sums[2].astype(BF16)
    from_end, from_own = across(sent_end), across(sent_own)
    down_end_grad = outward((sums[1] + from_end.astype(F32)).astype(BF16))
    down_own_grad = (sums[0] + from_own.astype(F32)).astype(BF16)
    down_grad = jnp.where(middle, down_own_grad, down_end_grad)

    latent_own = after(latent_bf[:rows], sent_end, sent_own)
    input_own = jnp.dot(latent_own, down_all, preferred_element_type=F32).astype(BF16)
    passed_own = shifted(after(input_own, from_end, passed_end), "section", -1)
    passed = jnp.where(middle, passed_own, passed_end)
    return (passed[None], down_grad[None], up_grad[None])


def solution(mesh):
    spec = P("section", "row", "col")
    folds = mesh.shape["row"] == 4 and mesh.shape["col"] == 2
    return jax.shard_map(
        folded_body if folds else general_body,
        mesh=mesh,
        in_specs=(spec,) * 4,
        out_specs=(spec,) * 3,
        check_vma=False,
    )
```

```python
import jax
import jax.numpy as jnp
from jax import lax
from jax.sharding import PartitionSpec as P

F32 = jnp.float32
BF16 = jnp.bfloat16


def shifted(value, axis, steps):
    count = lax.axis_size(axis)
    leading, last = (max(0, -steps), min(count, count - steps))
    return lax.ppermute(value, axis, [(source, source + steps) for source in range(leading, last)])


def general_body(inputs, down_weight, up_weight, value_grad):
    tokens = inputs[0]
    cotangent = value_grad[0]
    down_full = lax.all_gather(down_weight[0], "row", axis=0, tiled=True)
    up_full = lax.all_gather(up_weight[0], "row", axis=0, tiled=True)
    latent_part = jnp.einsum("td,ld->tl", tokens, down_full, preferred_element_type=F32)
    grad_part = jnp.einsum("tf,lf->tl", cotangent, up_full, preferred_element_type=F32)
    latent = lax.psum(latent_part.astype(BF16), "col").astype(F32)
    normed_grad = lax.psum(grad_part.astype(BF16), "col").astype(F32)
    inv_rms = lax.rsqrt(jnp.mean(latent * latent, axis=-1, keepdims=True) + 1e-06)
    normed = latent * inv_rms
    normed_bf = normed.astype(BF16)
    inner = jnp.mean(normed_grad * normed, axis=-1, keepdims=True)
    latent_bf = (inv_rms * (normed_grad - normed * inner)).astype(BF16)
    up_grad = lax.psum_scatter(
        jnp.einsum("tl,tf->lf", normed_bf, cotangent, preferred_element_type=F32).astype(BF16),
        "row",
        scatter_dimension=0,
        tiled=True,
    )
    down_grad = lax.psum_scatter(
        jnp.einsum("tl,td->ld", latent_bf, tokens, preferred_element_type=F32).astype(BF16),
        "row",
        scatter_dimension=0,
        tiled=True,
    )
    input_grad = jnp.einsum("tl,ld->td", latent_bf, down_full, preferred_element_type=F32)
    passed = shifted(input_grad.astype(BF16), "section", -1)
    return (passed[None], down_grad[None], up_grad[None])


def inward(value):
    return lax.ppermute(value, "row", [(0, 1), (3, 2)])


def across(value):
    return lax.ppermute(value, "row", [(1, 2), (2, 1)])


def outward(value):
    return lax.ppermute(value, "row", [(1, 0), (2, 3)])


def other_col(value):
    return lax.ppermute(value, "col", [(0, 1), (1, 0)])


def after(value, *earlier):
    return lax.optimization_barrier((value, *earlier))[0]


def rows_dot(left, right):
    return lax.dot_general(left, right, (((1,), (1,)), ((), ())), preferred_element_type=F32)


def tokens_dot(left, right):
    return lax.dot_general(left, right, (((0,), (0,)), ((), ())), preferred_element_type=F32)


def col_sum(part):
    sent = part.astype(BF16)
    return sent.astype(F32) + other_col(sent).astype(F32)


def folded_body(inputs, down_weight, up_weight, value_grad):
    tokens, down, up, cotangent = inputs[0], down_weight[0], up_weight[0], value_grad[0]
    rows = tokens.shape[0]
    lat = down.shape[0]
    feat = cotangent.shape[1]
    place = lax.axis_index("row")
    middle = (place == 1) | (place == 2)

    cut = feat // 2
    cuts = (slice(0, cut), slice(cut, feat))
    down_end = inward(down)
    tokens_end = inward(tokens)
    down_other = across(down)
    cot_other = across(cotangent)
    cot_end = [inward(cotangent[:, cuts[0]])]
    down_other_end = across(down_end)
    cot_end.append(inward(after(cotangent[:, cuts[1]], down_end, down_other)))
    cot_other_end = [across(cot_end[0])]
    up_end = inward(after(up, tokens_end, cot_end[0]))
    down_there = [outward(down), outward(down_other), outward(down_other_end)]

    tokens_mine = jnp.concatenate([tokens, after(tokens_end, down_there[0])], axis=0)
    down_all = jnp.concatenate([down, down_end, down_other, down_other_end], axis=0)
    down_used = jnp.where(
        middle,
        down_all,
        jnp.concatenate([down_there[0], down, down_there[1], down_there[2]], axis=0),
    )

    latent = col_sum(rows_dot(tokens_mine, down_all))
    inv_rms = lax.rsqrt(jnp.mean(latent * latent, axis=-1, keepdims=True) + 1e-06)
    normed = latent * inv_rms
    normed_bf = normed.astype(BF16)
    normed_sent = after(normed_bf[:, 2 * lat :], down_there[1])
    normed_other = across(normed_sent)
    normed_all = jnp.concatenate([normed_bf[:, : 2 * lat], normed_other], axis=0)

    cot_other_end.append(across(after(cot_end[1], normed_sent)))
    cot_all = [
        jnp.concatenate(
            [cotangent[:, cuts[k]], cot_end[k], cot_other[:, cuts[k]], cot_other_end[k]], axis=0
        )
        for k in range(2)
    ]

    up_first = tokens_dot(after(normed_all, down_there[2]), cot_all[0]).astype(BF16)
    back_first = outward(up_first[lat:])
    up_mine = jnp.concatenate([up, after(up_end, up_first, down_used)], axis=0)
    grad = rows_dot(cot_all[0], up_mine[:, cuts[0]]) + rows_dot(cot_all[1], up_mine[:, cuts[1]])
    grad = grad.astype(BF16)
    from_col = other_col(grad[2 * rows :])
    mine_from_col = other_col(grad[: 2 * rows])
    grad_other = grad[2 * rows :].astype(F32) + from_col.astype(F32)
    up_second = tokens_dot(normed_all, cot_all[1]).astype(BF16)
    back_second = outward(up_second[lat:])
    up_grad = jnp.concatenate(
        [
            jnp.where(middle, up_first[:lat], back_first),
            jnp.where(middle, up_second[:lat], back_second),
        ],
        axis=1,
    )

    grad_sent = after(grad_other.astype(BF16), up_second, back_first)
    grad_mine = grad[: 2 * rows].astype(F32) + after(mine_from_col, grad_sent).astype(F32)
    normed_grad = jnp.concatenate([grad_mine, across(grad_sent).astype(F32)], axis=1)
    inner = jnp.mean(normed_grad * normed, axis=-1, keepdims=True)
    latent_bf = (inv_rms * (normed_grad - normed * inner)).astype(BF16)
    latent_there = outward(latent_bf[rows:])
    latent_used = jnp.where(middle, latent_bf[:rows], latent_there)

    sums = [
        tokens_dot(latent_bf[:, j * lat : (j + 1) * lat], tokens_mine) for j in range(4)
    ]
    sent_end, sent_own = sums[3].astype(BF16), sums[2].astype(BF16)
    from_end, from_own = across(sent_end), across(after(sent_own, latent_there))
    down_end_grad = outward((sums[1] + from_end.astype(F32)).astype(BF16))
    down_own_grad = (sums[0] + from_own.astype(F32)).astype(BF16)
    down_grad = jnp.where(middle, down_own_grad, down_end_grad)

    input_grad = jnp.dot(latent_used, down_used, preferred_element_type=F32).astype(BF16)
    passed = shifted(input_grad, "section", -1)
    return (passed[None], down_grad[None], up_grad[None])


def solution(mesh):
    spec = P("section", "row", "col")
    folds = mesh.shape["row"] == 4 and mesh.shape["col"] == 2
    return jax.shard_map(
        folded_body if folds else general_body,
        mesh=mesh,
        in_specs=(spec,) * 4,
        out_specs=(spec,) * 3,
        check_vma=False,
    )
```

```python
import jax
import jax.numpy as jnp
from jax import lax
from jax.sharding import PartitionSpec as P

F32 = jnp.float32
BF16 = jnp.bfloat16


def shifted(value, axis, steps):
    count = lax.axis_size(axis)
    leading, last = (max(0, -steps), min(count, count - steps))
    return lax.ppermute(value, axis, [(source, source + steps) for source in range(leading, last)])


def general_body(inputs, down_weight, up_weight, value_grad):
    tokens = inputs[0]
    cotangent = value_grad[0]
    down_full = lax.all_gather(down_weight[0], "row", axis=0, tiled=True)
    up_full = lax.all_gather(up_weight[0], "row", axis=0, tiled=True)
    latent_part = jnp.einsum("td,ld->tl", tokens, down_full, preferred_element_type=F32)
    grad_part = jnp.einsum("tf,lf->tl", cotangent, up_full, preferred_element_type=F32)
    latent = lax.psum(latent_part.astype(BF16), "col").astype(F32)
    normed_grad = lax.psum(grad_part.astype(BF16), "col").astype(F32)
    inv_rms = lax.rsqrt(jnp.mean(latent * latent, axis=-1, keepdims=True) + 1e-06)
    normed = latent * inv_rms
    normed_bf = normed.astype(BF16)
    inner = jnp.mean(normed_grad * normed, axis=-1, keepdims=True)
    latent_bf = (inv_rms * (normed_grad - normed * inner)).astype(BF16)
    up_grad = lax.psum_scatter(
        jnp.einsum("tl,tf->lf", normed_bf, cotangent, preferred_element_type=F32).astype(BF16),
        "row",
        scatter_dimension=0,
        tiled=True,
    )
    down_grad = lax.psum_scatter(
        jnp.einsum("tl,td->ld", latent_bf, tokens, preferred_element_type=F32).astype(BF16),
        "row",
        scatter_dimension=0,
        tiled=True,
    )
    input_grad = jnp.einsum("tl,ld->td", latent_bf, down_full, preferred_element_type=F32)
    passed = shifted(input_grad.astype(BF16), "section", -1)
    return (passed[None], down_grad[None], up_grad[None])


def inward(value):
    return lax.ppermute(value, "row", [(0, 1), (3, 2)])


def across(value):
    return lax.ppermute(value, "row", [(1, 2), (2, 1)])


def outward(value):
    return lax.ppermute(value, "row", [(1, 0), (2, 3)])


def other_col(value):
    return lax.ppermute(value, "col", [(0, 1), (1, 0)])


def after(value, *earlier):
    return lax.optimization_barrier((value, *earlier))[0]


def rows_dot(left, right):
    return lax.dot_general(left, right, (((1,), (1,)), ((), ())), preferred_element_type=F32)


def tokens_dot(left, right):
    return lax.dot_general(left, right, (((0,), (0,)), ((), ())), preferred_element_type=F32)


def col_sum(part):
    sent = part.astype(BF16)
    return sent.astype(F32) + other_col(sent).astype(F32)


def folded_body(inputs, down_weight, up_weight, value_grad):
    tokens, down, up, cotangent = inputs[0], down_weight[0], up_weight[0], value_grad[0]
    rows = tokens.shape[0]
    lat = down.shape[0]
    feat = cotangent.shape[1]
    place = lax.axis_index("row")
    middle = (place == 1) | (place == 2)

    cut = feat // 2
    cuts = (slice(0, cut), slice(cut, feat))
    down_end = inward(down)
    tokens_end = inward(tokens)
    down_other = across(down)
    cot_other = across(cotangent)
    cot_end = [inward(cotangent[:, cuts[0]])]
    down_other_end = across(down_end)
    cot_end.append(inward(after(cotangent[:, cuts[1]], down_end, down_other)))
    cot_other_end = [across(cot_end[0])]
    up_end = inward(after(up, tokens_end, cot_end[0]))
    down_there = [outward(down), outward(down_other), outward(down_other_end)]

    tokens_mine = jnp.concatenate([tokens, after(tokens_end, down_there[0])], axis=0)
    down_all = jnp.concatenate([down, down_end, down_other, down_other_end], axis=0)
    down_used = jnp.where(
        middle,
        down_all,
        jnp.concatenate([down_there[0], down, down_there[1], down_there[2]], axis=0),
    )

    latent = col_sum(rows_dot(tokens_mine, down_all))
    inv_rms = lax.rsqrt(jnp.mean(latent * latent, axis=-1, keepdims=True) + 1e-06)
    normed = latent * inv_rms
    normed_bf = normed.astype(BF16)
    normed_sent = after(normed_bf[:, 2 * lat :], down_there[1])
    normed_other = across(normed_sent)
    normed_all = jnp.concatenate([normed_bf[:, : 2 * lat], normed_other], axis=0)

    cot_other_end.append(across(after(cot_end[1], normed_sent)))
    def early_rows(k):
        return jnp.concatenate([cotangent[:, cuts[k]], cot_end[k], cot_other[:, cuts[k]]], axis=0)

    values = jnp.concatenate([early_rows(0), cot_other_end[0]], axis=0)
    up_first = tokens_dot(after(normed_all, down_there[2]), values).astype(BF16)
    back_first = outward(up_first[lat:])
    up_mine = jnp.concatenate([up, after(up_end, up_first, down_used)], axis=0)
    grad = rows_dot(values, up_mine[:, cuts[0]])
    early = grad[: 3 * rows] + rows_dot(early_rows(1), up_mine[:, cuts[1]])
    early = early.astype(BF16)
    early_sum = early.astype(F32) + other_col(early).astype(F32)

    last = after(cot_other_end[1], early)
    late = col_sum(grad[3 * rows :] + rows_dot(last, up_mine[:, cuts[1]]))
    values = jnp.concatenate([early_rows(1), last], axis=0)
    up_second = tokens_dot(normed_all, values).astype(BF16)
    back_second = outward(up_second[lat:])
    up_grad = jnp.concatenate(
        [
            jnp.where(middle, up_first[:lat], back_first),
            jnp.where(middle, up_second[:lat], back_second),
        ],
        axis=1,
    )

    grad_sent = jnp.concatenate([early_sum[2 * rows :], late], axis=0).astype(BF16)
    from_across = across(after(grad_sent, up_second, back_first))
    normed_grad = jnp.concatenate([early_sum[: 2 * rows], from_across.astype(F32)], axis=1)
    inner = jnp.mean(normed_grad * normed, axis=-1, keepdims=True)
    latent_bf = (inv_rms * (normed_grad - normed * inner)).astype(BF16)
    latent_there = outward(latent_bf[rows:])
    latent_used = jnp.where(middle, latent_bf[:rows], latent_there)

    sums = [
        tokens_dot(latent_bf[:, j * lat : (j + 1) * lat], tokens_mine) for j in range(4)
    ]
    width = tokens.shape[1] // 2
    halves = (slice(0, width), slice(width, 2 * width))
    sent_end, sent_own = sums[3].astype(BF16), sums[2].astype(BF16)
    from_end = [across(sent_end[:, half]) for half in halves]
    from_own = across(after(sent_own, from_end[0]))
    end_first = (sums[1][:, halves[0]] + from_end[0].astype(F32)).astype(BF16)
    end_second = sums[1][:, halves[1]] + after(from_end[1], end_first).astype(F32)
    down_end_grad = jnp.concatenate([outward(end_first), outward(end_second.astype(BF16))], axis=1)
    down_own_grad = (sums[0] + from_own.astype(F32)).astype(BF16)
    down_grad = jnp.where(middle, down_own_grad, down_end_grad)

    input_grad = jnp.dot(latent_used, down_used, preferred_element_type=F32).astype(BF16)
    passed = shifted(input_grad, "section", -1)
    return (passed[None], down_grad[None], up_grad[None])


def solution(mesh):
    spec = P("section", "row", "col")
    folds = mesh.shape["row"] == 4 and mesh.shape["col"] == 2
    return jax.shard_map(
        folded_body if folds else general_body,
        mesh=mesh,
        in_specs=(spec,) * 4,
        out_specs=(spec,) * 3,
        check_vma=False,
    )
```

```python
import jax
import jax.numpy as jnp
from jax import lax
from jax.sharding import PartitionSpec as P

F32 = jnp.float32
BF16 = jnp.bfloat16


def shifted(value, axis, steps):
    count = lax.axis_size(axis)
    leading, last = (max(0, -steps), min(count, count - steps))
    return lax.ppermute(value, axis, [(source, source + steps) for source in range(leading, last)])


def general_body(inputs, down_weight, up_weight, value_grad):
    tokens = inputs[0]
    cotangent = value_grad[0]
    down_full = lax.all_gather(down_weight[0], "row", axis=0, tiled=True)
    up_full = lax.all_gather(up_weight[0], "row", axis=0, tiled=True)
    latent_part = jnp.einsum("td,ld->tl", tokens, down_full, preferred_element_type=F32)
    grad_part = jnp.einsum("tf,lf->tl", cotangent, up_full, preferred_element_type=F32)
    latent = lax.psum(latent_part.astype(BF16), "col").astype(F32)
    normed_grad = lax.psum(grad_part.astype(BF16), "col").astype(F32)
    inv_rms = lax.rsqrt(jnp.mean(latent * latent, axis=-1, keepdims=True) + 1e-06)
    normed = latent * inv_rms
    normed_bf = normed.astype(BF16)
    inner = jnp.mean(normed_grad * normed, axis=-1, keepdims=True)
    latent_bf = (inv_rms * (normed_grad - normed * inner)).astype(BF16)
    up_grad = lax.psum_scatter(
        jnp.einsum("tl,tf->lf", normed_bf, cotangent, preferred_element_type=F32).astype(BF16),
        "row",
        scatter_dimension=0,
        tiled=True,
    )
    down_grad = lax.psum_scatter(
        jnp.einsum("tl,td->ld", latent_bf, tokens, preferred_element_type=F32).astype(BF16),
        "row",
        scatter_dimension=0,
        tiled=True,
    )
    input_grad = jnp.einsum("tl,ld->td", latent_bf, down_full, preferred_element_type=F32)
    passed = shifted(input_grad.astype(BF16), "section", -1)
    return (passed[None], down_grad[None], up_grad[None])


def inward(value):
    return lax.ppermute(value, "row", [(0, 1), (3, 2)])


def across(value):
    return lax.ppermute(value, "row", [(1, 2), (2, 1)])


def outward(value):
    return lax.ppermute(value, "row", [(1, 0), (2, 3)])


def other_col(value):
    return lax.ppermute(value, "col", [(0, 1), (1, 0)])


def after(value, *earlier):
    return lax.optimization_barrier((value, *earlier))[0]


def rows_dot(left, right):
    return lax.dot_general(left, right, (((1,), (1,)), ((), ())), preferred_element_type=F32)


def tokens_dot(left, right):
    return lax.dot_general(left, right, (((0,), (0,)), ((), ())), preferred_element_type=F32)


def col_sum(part):
    sent = part.astype(BF16)
    return sent.astype(F32) + other_col(sent).astype(F32)


def folded_body(inputs, down_weight, up_weight, value_grad):
    tokens, down, up, cotangent = inputs[0], down_weight[0], up_weight[0], value_grad[0]
    rows = tokens.shape[0]
    lat = down.shape[0]
    feat = cotangent.shape[1]
    place = lax.axis_index("row")
    middle = (place == 1) | (place == 2)

    cut = feat // 2
    cuts = (slice(0, cut), slice(cut, feat))
    down_end = inward(down)
    tokens_end = inward(tokens)
    down_other = across(down)
    cot_other = across(cotangent)
    cot_end = [inward(cotangent[:, cuts[0]])]
    down_other_end = across(down_end)
    cot_end.append(inward(after(cotangent[:, cuts[1]], down_end, down_other)))
    cot_other_end = [across(cot_end[0])]
    up_end = inward(after(up, tokens_end, cot_end[0]))
    down_there = [outward(down), outward(down_other), outward(down_other_end)]

    tokens_mine = jnp.concatenate([tokens, after(tokens_end, down_there[0])], axis=0)
    down_all = jnp.concatenate([down, down_end, down_other, down_other_end], axis=0)
    down_used = jnp.where(
        middle,
        down_all,
        jnp.concatenate([down_there[0], down, down_there[1], down_there[2]], axis=0),
    )

    latent = col_sum(rows_dot(tokens_mine, down_all))
    inv_rms = lax.rsqrt(jnp.mean(latent * latent, axis=-1, keepdims=True) + 1e-06)
    normed = latent * inv_rms
    normed_bf = normed.astype(BF16)
    normed_sent = after(normed_bf[:, 2 * lat :], down_there[1])
    normed_other = across(normed_sent)
    normed_all = jnp.concatenate([normed_bf[:, : 2 * lat], normed_other], axis=0)

    cot_other_end.append(across(after(cot_end[1], normed_sent)))
    def early_rows(k):
        return jnp.concatenate([cotangent[:, cuts[k]], cot_end[k], cot_other[:, cuts[k]]], axis=0)

    values = jnp.concatenate([early_rows(0), cot_other_end[0]], axis=0)
    up_first = tokens_dot(after(normed_all, down_there[2]), values).astype(BF16)
    back_first = outward(up_first[lat:])
    up_mine = jnp.concatenate([up, after(up_end, up_first, down_used)], axis=0)
    grad = rows_dot(values, up_mine[:, cuts[0]])
    early = grad[: 3 * rows] + rows_dot(early_rows(1), up_mine[:, cuts[1]])
    early = early.astype(BF16)
    early_sum = early.astype(F32) + other_col(early).astype(F32)

    last = after(cot_other_end[1], early)
    late = col_sum(grad[3 * rows :] + rows_dot(last, up_mine[:, cuts[1]]))
    values = jnp.concatenate([early_rows(1), last], axis=0)
    up_second = tokens_dot(normed_all, values).astype(BF16)
    back_second = outward(up_second[lat:])
    up_grad = jnp.concatenate(
        [
            jnp.where(middle, up_first[:lat], back_first),
            jnp.where(middle, up_second[:lat], back_second),
        ],
        axis=1,
    )

    grad_sent = jnp.concatenate([early_sum[2 * rows :], late], axis=0).astype(BF16)
    from_across = across(after(grad_sent, up_second, back_first))
    normed_grad = jnp.concatenate([early_sum[: 2 * rows], from_across.astype(F32)], axis=1)
    inner = jnp.mean(normed_grad * normed, axis=-1, keepdims=True)
    latent_bf = (inv_rms * (normed_grad - normed * inner)).astype(BF16)

    sums = [
        tokens_dot(latent_bf[:, j * lat : (j + 1) * lat], tokens_mine) for j in range(4)
    ]
    width = tokens.shape[1] // 2
    halves = (slice(0, width), slice(width, 2 * width))
    sent_end, sent_own = sums[3].astype(BF16), sums[2].astype(BF16)
    from_end = [across(sent_end[:, half]) for half in halves]
    latent_there = outward(after(latent_bf[rows:], sent_end, sent_own))
    latent_used = jnp.where(middle, latent_bf[:rows], latent_there)
    end_first = (sums[1][:, halves[0]] + from_end[0].astype(F32)).astype(BF16)
    from_own = across(after(sent_own, end_first))
    end_second = sums[1][:, halves[1]] + after(from_end[1], end_first).astype(F32)
    down_end_grad = jnp.concatenate([outward(end_first), outward(end_second.astype(BF16))], axis=1)
    input_grad = jnp.dot(latent_used, down_used, preferred_element_type=F32).astype(BF16)
    passed = shifted(input_grad, "section", -1)
    final = lax.axis_index("section") == lax.axis_size("section") - 1
    passed = jnp.where(final, jnp.zeros_like(passed), passed)
    down_own_grad = (sums[0] + after(from_own, passed).astype(F32)).astype(BF16)
    down_grad = jnp.where(middle, down_own_grad, down_end_grad)
    return (passed[None], down_grad[None], up_grad[None])


def solution(mesh):
    spec = P("section", "row", "col")
    folds = mesh.shape["row"] == 4 and mesh.shape["col"] == 2
    return jax.shard_map(
        folded_body if folds else general_body,
        mesh=mesh,
        in_specs=(spec,) * 4,
        out_specs=(spec,) * 3,
        check_vma=False,
    )
```

```python
import jax
import jax.numpy as jnp
from jax import lax
from jax.sharding import PartitionSpec as P

F32 = jnp.float32
BF16 = jnp.bfloat16


def shifted(value, axis, steps):
    count = lax.axis_size(axis)
    leading, last = (max(0, -steps), min(count, count - steps))
    return lax.ppermute(value, axis, [(source, source + steps) for source in range(leading, last)])


def general_body(inputs, down_weight, up_weight, value_grad):
    tokens = inputs[0]
    cotangent = value_grad[0]
    down_full = lax.all_gather(down_weight[0], "row", axis=0, tiled=True)
    up_full = lax.all_gather(up_weight[0], "row", axis=0, tiled=True)
    latent_part = jnp.einsum("td,ld->tl", tokens, down_full, preferred_element_type=F32)
    grad_part = jnp.einsum("tf,lf->tl", cotangent, up_full, preferred_element_type=F32)
    latent = lax.psum(latent_part.astype(BF16), "col").astype(F32)
    normed_grad = lax.psum(grad_part.astype(BF16), "col").astype(F32)
    inv_rms = lax.rsqrt(jnp.mean(latent * latent, axis=-1, keepdims=True) + 1e-06)
    normed = latent * inv_rms
    normed_bf = normed.astype(BF16)
    inner = jnp.mean(normed_grad * normed, axis=-1, keepdims=True)
    latent_bf = (inv_rms * (normed_grad - normed * inner)).astype(BF16)
    up_grad = lax.psum_scatter(
        jnp.einsum("tl,tf->lf", normed_bf, cotangent, preferred_element_type=F32).astype(BF16),
        "row",
        scatter_dimension=0,
        tiled=True,
    )
    down_grad = lax.psum_scatter(
        jnp.einsum("tl,td->ld", latent_bf, tokens, preferred_element_type=F32).astype(BF16),
        "row",
        scatter_dimension=0,
        tiled=True,
    )
    input_grad = jnp.einsum("tl,ld->td", latent_bf, down_full, preferred_element_type=F32)
    passed = shifted(input_grad.astype(BF16), "section", -1)
    return (passed[None], down_grad[None], up_grad[None])


def inward(value):
    return lax.ppermute(value, "row", [(0, 1), (3, 2)])


def across(value):
    return lax.ppermute(value, "row", [(1, 2), (2, 1)])


def outward(value):
    return lax.ppermute(value, "row", [(1, 0), (2, 3)])


def other_col(value):
    return lax.ppermute(value, "col", [(0, 1), (1, 0)])


def after(value, *earlier):
    return lax.optimization_barrier((value, *earlier))[0]


def rows_dot(left, right):
    return lax.dot_general(left, right, (((1,), (1,)), ((), ())), preferred_element_type=F32)


def tokens_dot(left, right):
    return lax.dot_general(left, right, (((0,), (0,)), ((), ())), preferred_element_type=F32)


def col_sum(part):
    sent = part.astype(BF16)
    return sent.astype(F32) + other_col(sent).astype(F32)


def folded_body(inputs, down_weight, up_weight, value_grad):
    tokens, down, up, cotangent = inputs[0], down_weight[0], up_weight[0], value_grad[0]
    rows = tokens.shape[0]
    lat = down.shape[0]
    feat = cotangent.shape[1]
    place = lax.axis_index("row")
    middle = (place == 1) | (place == 2)

    cut = feat // 2
    cuts = (slice(0, cut), slice(cut, feat))
    down_end = inward(down)
    tokens_end = inward(tokens)
    down_other = across(down)
    cot_other = across(cotangent)
    cot_end = [inward(cotangent[:, cuts[0]])]
    down_other_end = across(down_end)
    cot_end.append(inward(after(cotangent[:, cuts[1]], down_end, down_other)))
    cot_other_end = [across(cot_end[0])]
    up_end = inward(after(up, tokens_end, cot_end[0]))
    down_there = [outward(down), outward(down_other), outward(down_other_end)]

    tokens_mine = jnp.concatenate([tokens, after(tokens_end, down_there[0])], axis=0)
    down_all = jnp.concatenate([down, down_end, down_other, down_other_end], axis=0)
    down_used = jnp.where(
        middle,
        down_all,
        jnp.concatenate([down_there[0], down, down_there[1], down_there[2]], axis=0),
    )

    latent = col_sum(rows_dot(tokens_mine, down_all))
    inv_rms = lax.rsqrt(jnp.mean(latent * latent, axis=-1, keepdims=True) + 1e-06)
    def parts(value):
        high = value.astype(BF16)
        return [high, (value - high.astype(F32)).astype(BF16)]

    normed = latent * inv_rms
    normed_bf = normed.astype(BF16)
    inv_parts = parts(inv_rms)
    normed_sent = after(normed_bf[:, 2 * lat :], down_there[1], *inv_parts)
    normed_other = across(normed_sent)
    normed_all = jnp.concatenate([normed_bf[:, : 2 * lat], normed_other], axis=0)

    cot_other_end.append(across(after(cot_end[1], normed_sent)))
    def early_rows(k):
        return jnp.concatenate([cotangent[:, cuts[k]], cot_end[k], cot_other[:, cuts[k]]], axis=0)

    values = jnp.concatenate([early_rows(0), cot_other_end[0]], axis=0)
    up_first = tokens_dot(after(normed_all, down_there[2]), values).astype(BF16)
    back_first = outward(up_first[lat:])
    up_mine = jnp.concatenate([up, after(up_end, up_first, down_used)], axis=0)
    grad = rows_dot(values, up_mine[:, cuts[0]])
    early = grad[: 3 * rows] + rows_dot(early_rows(1), up_mine[:, cuts[1]])
    early = early.astype(BF16)
    early_sum = early.astype(F32) + other_col(early).astype(F32)

    last = after(cot_other_end[1], early)
    late = (grad[3 * rows :] + rows_dot(last, up_mine[:, cuts[1]])).astype(BF16)
    early_mine = after(early_sum[: 2 * rows], late)
    late = late.astype(F32) + other_col(late).astype(F32)
    values = jnp.concatenate([early_rows(1), last], axis=0)
    up_second = tokens_dot(normed_all, values).astype(BF16)
    back_second = outward(up_second[lat:])
    up_grad = jnp.concatenate(
        [
            jnp.where(middle, up_first[:lat], back_first),
            jnp.where(middle, up_second[:lat], back_second),
        ],
        axis=1,
    )

    width = tokens.shape[1]
    first, share = width // 10 // 128 * 128, 3 * width // 10 // 128 * 128
    half = (share + width) // 2 // 128 * 128
    moved_first = across(tokens_mine[:, :first])

    row_sum = jnp.sum(early_mine * normed[:, : 2 * lat], axis=-1, keepdims=True)
    riders = parts(row_sum) + inv_parts
    riders.append(jnp.zeros((2 * rows, 124), BF16))
    grad_other = jnp.concatenate([early_sum[2 * rows :], late], axis=0)
    grad_sent = jnp.concatenate([grad_other.astype(BF16)] + riders, axis=1)
    grad_sent = after(grad_sent, up_second, back_first, moved_first)
    moved_second = across(after(tokens_mine[:, first:share], grad_sent))
    from_across = across(grad_sent).astype(F32)
    normed_grad = jnp.concatenate([early_mine, from_across[:, : 2 * lat]], axis=1)
    inner = jnp.mean(normed_grad * normed, axis=-1, keepdims=True)
    latent_bf = (inv_rms * (normed_grad - normed * inner)).astype(BF16)
    latent_there = outward(latent_bf[rows:])
    latent_used = jnp.where(middle, latent_bf[:rows], latent_there)

    sums = [
        tokens_dot(latent_bf[:, j * lat : (j + 1) * lat], tokens_mine[:, share:]) for j in range(4)
    ]
    sent_end, sent_own = sums[3].astype(BF16), sums[2].astype(BF16)
    from_end = [across(sent_end[:, : half - share]), across(sent_end[:, half - share :])]

    riders = from_across[:, 2 * lat : 2 * lat + 4]
    row_sum_other, inv_rms_other = riders[:, :1] + riders[:, 1:2], riders[:, 2:3] + riders[:, 3:]
    values = normed_other.astype(F32)
    inner = row_sum_other + jnp.sum(grad_other * values, axis=-1, keepdims=True)
    inner = inner / (4 * lat)
    latent_other = (inv_rms_other * (grad_other - values * inner)).astype(BF16)
    moved = jnp.concatenate([moved_first, moved_second], axis=1)
    direct = tokens_dot(
        jnp.concatenate([latent_bf[:, : 2 * lat], latent_other], axis=0),
        jnp.concatenate([tokens_mine[:, :share], moved], axis=0),
    ).astype(BF16)

    from_own = across(after(sent_own, from_end[0], direct))
    end_first = (sums[1][:, : half - share] + from_end[0].astype(F32)).astype(BF16)
    end_second = sums[1][:, half - share :] + after(from_end[1], end_first).astype(F32)
    down_end_grad = jnp.concatenate(
        [outward(direct[lat:]), outward(end_first), outward(end_second.astype(BF16))], axis=1
    )

    input_grad = jnp.dot(latent_used, down_used, preferred_element_type=F32).astype(BF16)
    passed = shifted(input_grad, "section", -1)
    final = lax.axis_index("section") == lax.axis_size("section") - 1
    passed = jnp.where(final, jnp.zeros_like(passed), passed)
    own_rest = (sums[0] + after(from_own, passed).astype(F32)).astype(BF16)
    down_grad = jnp.where(middle, jnp.concatenate([direct[:lat], own_rest], axis=1), down_end_grad)
    return (passed[None], down_grad[None], up_grad[None])


def solution(mesh):
    spec = P("section", "row", "col")
    folds = mesh.shape["row"] == 4 and mesh.shape["col"] == 2
    return jax.shard_map(
        folded_body if folds else general_body,
        mesh=mesh,
        in_specs=(spec,) * 4,
        out_specs=(spec,) * 3,
        check_vma=False,
    )
```

```python
import jax
import jax.numpy as jnp
from jax import lax
from jax.sharding import PartitionSpec as P

F32 = jnp.float32
BF16 = jnp.bfloat16


def shifted(value, axis, steps):
    count = lax.axis_size(axis)
    leading, last = (max(0, -steps), min(count, count - steps))
    return lax.ppermute(value, axis, [(source, source + steps) for source in range(leading, last)])


def general_body(inputs, down_weight, up_weight, value_grad):
    tokens = inputs[0]
    cotangent = value_grad[0]
    down_full = lax.all_gather(down_weight[0], "row", axis=0, tiled=True)
    up_full = lax.all_gather(up_weight[0], "row", axis=0, tiled=True)
    latent_part = jnp.einsum("td,ld->tl", tokens, down_full, preferred_element_type=F32)
    grad_part = jnp.einsum("tf,lf->tl", cotangent, up_full, preferred_element_type=F32)
    latent = lax.psum(latent_part.astype(BF16), "col").astype(F32)
    normed_grad = lax.psum(grad_part.astype(BF16), "col").astype(F32)
    inv_rms = lax.rsqrt(jnp.mean(latent * latent, axis=-1, keepdims=True) + 1e-06)
    normed = latent * inv_rms
    normed_bf = normed.astype(BF16)
    inner = jnp.mean(normed_grad * normed, axis=-1, keepdims=True)
    latent_bf = (inv_rms * (normed_grad - normed * inner)).astype(BF16)
    up_grad = lax.psum_scatter(
        jnp.einsum("tl,tf->lf", normed_bf, cotangent, preferred_element_type=F32).astype(BF16),
        "row",
        scatter_dimension=0,
        tiled=True,
    )
    down_grad = lax.psum_scatter(
        jnp.einsum("tl,td->ld", latent_bf, tokens, preferred_element_type=F32).astype(BF16),
        "row",
        scatter_dimension=0,
        tiled=True,
    )
    input_grad = jnp.einsum("tl,ld->td", latent_bf, down_full, preferred_element_type=F32)
    passed = shifted(input_grad.astype(BF16), "section", -1)
    return (passed[None], down_grad[None], up_grad[None])


def inward(value):
    return lax.ppermute(value, "row", [(0, 1), (3, 2)])


def across(value):
    return lax.ppermute(value, "row", [(1, 2), (2, 1)])


def outward(value):
    return lax.ppermute(value, "row", [(1, 0), (2, 3)])


def other_col(value):
    return lax.ppermute(value, "col", [(0, 1), (1, 0)])


def after(value, *earlier):
    return lax.optimization_barrier((value, *earlier))[0]


def across_other_col(value):
    pairs = [(2 * a + c, 2 * b + 1 - c) for a, b in ((1, 2), (2, 1)) for c in range(2)]
    return lax.ppermute(value, ("row", "col"), pairs)


def rows_dot(left, right):
    return lax.dot_general(left, right, (((1,), (1,)), ((), ())), preferred_element_type=F32)


def tokens_dot(left, right):
    return lax.dot_general(left, right, (((0,), (0,)), ((), ())), preferred_element_type=F32)


def col_sum(part):
    sent = part.astype(BF16)
    return sent.astype(F32) + other_col(sent).astype(F32)


def folded_body(inputs, down_weight, up_weight, value_grad):
    tokens, down, up, cotangent = inputs[0], down_weight[0], up_weight[0], value_grad[0]
    rows = tokens.shape[0]
    lat = down.shape[0]
    feat = cotangent.shape[1]
    place = lax.axis_index("row")
    middle = (place == 1) | (place == 2)

    cut = feat // 2
    cuts = (slice(0, cut), slice(cut, feat))
    down_end = inward(down)
    tokens_end = inward(tokens)
    down_other = across(down)
    cot_other = across(cotangent)
    cot_end = [inward(cotangent[:, cuts[0]])]
    down_other_end = across(down_end)
    cot_end.append(inward(after(cotangent[:, cuts[1]], down_end, down_other)))
    cot_other_end = [across(cot_end[0])]
    up_end = inward(after(up, tokens_end, cot_end[0]))
    down_there = [outward(down), outward(down_other), outward(down_other_end)]

    tokens_mine = jnp.concatenate([tokens, after(tokens_end, down_there[0])], axis=0)
    down_all = jnp.concatenate([down, down_end, down_other, down_other_end], axis=0)
    down_used = jnp.where(
        middle,
        down_all,
        jnp.concatenate([down_there[0], down, down_there[1], down_there[2]], axis=0),
    )

    latent = col_sum(rows_dot(tokens_mine, down_all))
    inv_rms = lax.rsqrt(jnp.mean(latent * latent, axis=-1, keepdims=True) + 1e-06)
    normed = latent * inv_rms
    normed_bf = normed.astype(BF16)
    normed_sent = after(normed_bf[:, 2 * lat :], down_there[1])
    normed_other = across(normed_sent)
    normed_all = jnp.concatenate([normed_bf[:, : 2 * lat], normed_other], axis=0)

    cot_other_end.append(across(after(cot_end[1], normed_sent)))
    def early_rows(k):
        return jnp.concatenate([cotangent[:, cuts[k]], cot_end[k], cot_other[:, cuts[k]]], axis=0)

    values = jnp.concatenate([early_rows(0), cot_other_end[0]], axis=0)
    up_first = tokens_dot(after(normed_all, down_there[2]), values).astype(BF16)
    back_first = outward(up_first[lat:])
    up_mine = jnp.concatenate([up, after(up_end, up_first, down_used)], axis=0)
    grad = rows_dot(values, up_mine[:, cuts[0]])
    early = grad[: 3 * rows] + rows_dot(early_rows(1), up_mine[:, cuts[1]])
    early = early.astype(BF16)
    early_sum = early.astype(F32) + other_col(early).astype(F32)

    last = after(cot_other_end[1], early)
    late = (grad[3 * rows :] + rows_dot(last, up_mine[:, cuts[1]])).astype(BF16)
    straight = across(jnp.concatenate([early_sum[2 * rows :].astype(BF16), late], axis=0))
    crossed = across_other_col(late)
    values = jnp.concatenate([early_rows(1), after(last, late)], axis=0)
    up_second = tokens_dot(normed_all, values).astype(BF16)
    back_second = outward(up_second[lat:])
    up_grad = jnp.concatenate(
        [
            jnp.where(middle, up_first[:lat], back_first),
            jnp.where(middle, up_second[:lat], back_second),
        ],
        axis=1,
    )

    straight = after(straight, up_second, back_first).astype(F32)
    from_across = jnp.concatenate(
        [straight[:rows], straight[rows:] + crossed.astype(F32)], axis=0
    )
    normed_grad = jnp.concatenate([early_sum[: 2 * rows], from_across], axis=1)
    inner = jnp.mean(normed_grad * normed, axis=-1, keepdims=True)
    latent_bf = (inv_rms * (normed_grad - normed * inner)).astype(BF16)
    latent_there = outward(latent_bf[rows:])
    latent_used = jnp.where(middle, latent_bf[:rows], latent_there)

    sums = [
        tokens_dot(latent_bf[:, j * lat : (j + 1) * lat], tokens_mine).astype(BF16)
        for j in range(4)
    ]
    width = tokens.shape[1] // 2
    halves = (slice(0, width), slice(width, 2 * width))
    sent_end, sent_own = sums[3], sums[2]
    from_end = [across(sent_end[:, half]) for half in halves]
    from_own = across(after(sent_own, from_end[0]))
    end_first = (sums[1][:, halves[0]] + from_end[0].astype(F32)).astype(BF16)
    end_second = sums[1][:, halves[1]] + after(from_end[1], end_first).astype(F32)
    down_end_grad = jnp.concatenate([outward(end_first), outward(end_second.astype(BF16))], axis=1)

    input_grad = jnp.dot(latent_used, down_used, preferred_element_type=F32).astype(BF16)
    passed = shifted(input_grad, "section", -1)
    down_own_grad = (sums[0] + after(from_own, passed).astype(F32)).astype(BF16)
    down_grad = jnp.where(middle, down_own_grad, down_end_grad)
    return (passed[None], down_grad[None], up_grad[None])


def solution(mesh):
    spec = P("section", "row", "col")
    folds = mesh.shape["row"] == 4 and mesh.shape["col"] == 2
    return jax.shard_map(
        folded_body if folds else general_body,
        mesh=mesh,
        in_specs=(spec,) * 4,
        out_specs=(spec,) * 3,
        check_vma=False,
    )
```

```python
import jax
import jax.numpy as jnp
from jax import lax
from jax.sharding import PartitionSpec as P

F32 = jnp.float32
BF16 = jnp.bfloat16


def shifted(value, axis, steps):
    count = lax.axis_size(axis)
    leading, last = (max(0, -steps), min(count, count - steps))
    return lax.ppermute(value, axis, [(source, source + steps) for source in range(leading, last)])


def general_body(inputs, down_weight, up_weight, value_grad):
    tokens = inputs[0]
    cotangent = value_grad[0]
    down_full = lax.all_gather(down_weight[0], "row", axis=0, tiled=True)
    up_full = lax.all_gather(up_weight[0], "row", axis=0, tiled=True)
    latent_part = jnp.einsum("td,ld->tl", tokens, down_full, preferred_element_type=F32)
    grad_part = jnp.einsum("tf,lf->tl", cotangent, up_full, preferred_element_type=F32)
    latent = lax.psum(latent_part.astype(BF16), "col").astype(F32)
    normed_grad = lax.psum(grad_part.astype(BF16), "col").astype(F32)
    inv_rms = lax.rsqrt(jnp.mean(latent * latent, axis=-1, keepdims=True) + 1e-06)
    normed = latent * inv_rms
    normed_bf = normed.astype(BF16)
    inner = jnp.mean(normed_grad * normed, axis=-1, keepdims=True)
    latent_bf = (inv_rms * (normed_grad - normed * inner)).astype(BF16)
    up_grad = lax.psum_scatter(
        jnp.einsum("tl,tf->lf", normed_bf, cotangent, preferred_element_type=F32).astype(BF16),
        "row",
        scatter_dimension=0,
        tiled=True,
    )
    down_grad = lax.psum_scatter(
        jnp.einsum("tl,td->ld", latent_bf, tokens, preferred_element_type=F32).astype(BF16),
        "row",
        scatter_dimension=0,
        tiled=True,
    )
    input_grad = jnp.einsum("tl,ld->td", latent_bf, down_full, preferred_element_type=F32)
    passed = shifted(input_grad.astype(BF16), "section", -1)
    return (passed[None], down_grad[None], up_grad[None])


def inward(value):
    return lax.ppermute(value, "row", [(0, 1), (3, 2)])


def across(value):
    return lax.ppermute(value, "row", [(1, 2), (2, 1)])


def outward(value):
    return lax.ppermute(value, "row", [(1, 0), (2, 3)])


def other_col(value):
    return lax.ppermute(value, "col", [(0, 1), (1, 0)])


def after(value, *earlier):
    return lax.optimization_barrier((value, *earlier))[0]


def rows_dot(left, right):
    return lax.dot_general(left, right, (((1,), (1,)), ((), ())), preferred_element_type=F32)


def tokens_dot(left, right):
    return lax.dot_general(left, right, (((0,), (0,)), ((), ())), preferred_element_type=F32)


def col_sum(part):
    sent = part.astype(BF16)
    return sent.astype(F32) + other_col(sent).astype(F32)


def folded_body(inputs, down_weight, up_weight, value_grad):
    tokens, down, up, cotangent = inputs[0], down_weight[0], up_weight[0], value_grad[0]
    rows = tokens.shape[0]
    lat = down.shape[0]
    feat = cotangent.shape[1]
    place = lax.axis_index("row")
    middle = (place == 1) | (place == 2)

    cut = feat // 2
    cuts = (slice(0, cut), slice(cut, feat))
    down_end = inward(down)
    tokens_end = inward(tokens)
    down_other = across(down)
    cot_other = across(cotangent)
    cot_end = [inward(cotangent[:, cuts[0]])]
    down_other_end = across(down_end)
    cot_end.append(inward(after(cotangent[:, cuts[1]], down_end, down_other)))
    cot_other_end = [across(cot_end[0])]
    up_end = inward(after(up, tokens_end, cot_end[0]))
    down_there = [outward(down), outward(down_other), outward(down_other_end)]

    tokens_mine = jnp.concatenate([tokens, after(tokens_end, down_there[0])], axis=0)
    down_all = jnp.concatenate([down, down_end, down_other, down_other_end], axis=0)
    down_used = jnp.where(
        middle,
        down_all,
        jnp.concatenate([down_there[0], down, down_there[1], down_there[2]], axis=0),
    )

    latent = col_sum(rows_dot(tokens_mine, down_all))
    inv_rms = lax.rsqrt(jnp.mean(latent * latent, axis=-1, keepdims=True) + 1e-06)
    normed = latent * inv_rms
    normed_bf = normed.astype(BF16)
    normed_sent = after(normed_bf[:, 2 * lat :], down_there[1])
    normed_other = across(normed_sent)
    normed_all = jnp.concatenate([normed_bf[:, : 2 * lat], normed_other], axis=0)

    cot_other_end.append(across(after(cot_end[1], normed_sent)))
    def early_rows(k):
        return jnp.concatenate([cotangent[:, cuts[k]], cot_end[k], cot_other[:, cuts[k]]], axis=0)

    values = jnp.concatenate([early_rows(0), cot_other_end[0]], axis=0)
    up_first = tokens_dot(after(normed_all, down_there[2]), values).astype(BF16)
    back_first = outward(up_first[lat:])
    up_mine = jnp.concatenate([up, after(up_end, up_first, down_used)], axis=0)
    grad = rows_dot(values, up_mine[:, cuts[0]])
    early = grad[: 3 * rows] + rows_dot(early_rows(1), up_mine[:, cuts[1]])
    early = early.astype(BF16)
    early_sum = early.astype(F32) + other_col(early).astype(F32)

    last = after(cot_other_end[1], early)
    late = col_sum(grad[3 * rows :] + rows_dot(last, up_mine[:, cuts[1]]))
    values = jnp.concatenate([early_rows(1), last], axis=0)
    up_second = tokens_dot(normed_all, values).astype(BF16)
    back_second = outward(up_second[lat:])
    up_grad = jnp.concatenate(
        [
            jnp.where(middle, up_first[:lat], back_first),
            jnp.where(middle, up_second[:lat], back_second),
        ],
        axis=1,
    )

    grad_sent = jnp.concatenate([early_sum[2 * rows :], late], axis=0).astype(BF16)
    from_across = across(after(grad_sent, up_second, back_first))
    normed_grad = jnp.concatenate([early_sum[: 2 * rows], from_across.astype(F32)], axis=1)
    inner = jnp.mean(normed_grad * normed, axis=-1, keepdims=True)
    latent_bf = (inv_rms * (normed_grad - normed * inner)).astype(BF16)
    latent_there = outward(latent_bf[rows:])
    latent_used = jnp.where(middle, latent_bf[:rows], latent_there)

    sums = [
        tokens_dot(latent_bf[:, j * lat : (j + 1) * lat], tokens_mine).astype(BF16)
        for j in range(4)
    ]
    width = tokens.shape[1] // 2
    halves = (slice(0, width), slice(width, 2 * width))
    sent_end, sent_own = sums[3], sums[2]
    from_end = [across(sent_end[:, half]) for half in halves]
    end_first = (sums[1][:, halves[0]] + from_end[0].astype(F32)).astype(BF16)
    from_own = across(after(sent_own, end_first))
    end_second = sums[1][:, halves[1]] + after(from_end[1], end_first).astype(F32)
    down_end_grad = jnp.concatenate([outward(end_first), outward(end_second.astype(BF16))], axis=1)
    input_grad = jnp.dot(latent_used, down_used, preferred_element_type=F32).astype(BF16)
    passed = shifted(input_grad, "section", -1)
    final = lax.axis_index("section") == lax.axis_size("section") - 1
    passed = jnp.where(final, jnp.zeros_like(passed), passed)
    down_own_grad = (sums[0] + after(from_own, passed).astype(F32)).astype(BF16)
    down_grad = jnp.where(middle, down_own_grad, down_end_grad)
    return (passed[None], down_grad[None], up_grad[None])


def solution(mesh):
    spec = P("section", "row", "col")
    folds = mesh.shape["row"] == 4 and mesh.shape["col"] == 2
    return jax.shard_map(
        folded_body if folds else general_body,
        mesh=mesh,
        in_specs=(spec,) * 4,
        out_specs=(spec,) * 3,
        check_vma=False,
    )
```

```python
import jax
import jax.numpy as jnp
from jax import lax
from jax.sharding import PartitionSpec as P

F32 = jnp.float32
BF16 = jnp.bfloat16


def shifted(value, axis, steps):
    count = lax.axis_size(axis)
    leading, last = (max(0, -steps), min(count, count - steps))
    return lax.ppermute(value, axis, [(source, source + steps) for source in range(leading, last)])


def general_body(inputs, down_weight, up_weight, value_grad):
    tokens = inputs[0]
    cotangent = value_grad[0]
    down_full = lax.all_gather(down_weight[0], "row", axis=0, tiled=True)
    up_full = lax.all_gather(up_weight[0], "row", axis=0, tiled=True)
    latent_part = jnp.einsum("td,ld->tl", tokens, down_full, preferred_element_type=F32)
    grad_part = jnp.einsum("tf,lf->tl", cotangent, up_full, preferred_element_type=F32)
    latent = lax.psum(latent_part.astype(BF16), "col").astype(F32)
    normed_grad = lax.psum(grad_part.astype(BF16), "col").astype(F32)
    inv_rms = lax.rsqrt(jnp.mean(latent * latent, axis=-1, keepdims=True) + 1e-06)
    normed = latent * inv_rms
    normed_bf = normed.astype(BF16)
    inner = jnp.mean(normed_grad * normed, axis=-1, keepdims=True)
    latent_bf = (inv_rms * (normed_grad - normed * inner)).astype(BF16)
    up_grad = lax.psum_scatter(
        jnp.einsum("tl,tf->lf", normed_bf, cotangent, preferred_element_type=F32).astype(BF16),
        "row",
        scatter_dimension=0,
        tiled=True,
    )
    down_grad = lax.psum_scatter(
        jnp.einsum("tl,td->ld", latent_bf, tokens, preferred_element_type=F32).astype(BF16),
        "row",
        scatter_dimension=0,
        tiled=True,
    )
    input_grad = jnp.einsum("tl,ld->td", latent_bf, down_full, preferred_element_type=F32)
    passed = shifted(input_grad.astype(BF16), "section", -1)
    return (passed[None], down_grad[None], up_grad[None])


def inward(value):
    return lax.ppermute(value, "row", [(0, 1), (3, 2)])


def across(value):
    return lax.ppermute(value, "row", [(1, 2), (2, 1)])


def outward(value):
    return lax.ppermute(value, "row", [(1, 0), (2, 3)])


def other_col(value):
    return lax.ppermute(value, "col", [(0, 1), (1, 0)])


def after(value, *earlier):
    return lax.optimization_barrier((value, *earlier))[0]


def rows_dot(left, right):
    return lax.dot_general(left, right, (((1,), (1,)), ((), ())), preferred_element_type=F32)


def tokens_dot(left, right):
    return lax.dot_general(left, right, (((0,), (0,)), ((), ())), preferred_element_type=F32)


def col_sum(part):
    sent = part.astype(BF16)
    return sent.astype(F32) + other_col(sent).astype(F32)


def folded_body(inputs, down_weight, up_weight, value_grad):
    tokens, down, up, cotangent = inputs[0], down_weight[0], up_weight[0], value_grad[0]
    rows = tokens.shape[0]
    lat = down.shape[0]
    feat = cotangent.shape[1]
    place = lax.axis_index("row")
    middle = (place == 1) | (place == 2)

    cut = feat // 2
    cuts = (slice(0, cut), slice(cut, feat))
    down_end = inward(down)
    tokens_end = inward(tokens)
    down_other = across(down)
    cot_other = across(cotangent)
    cot_end = [inward(cotangent[:, cuts[0]])]
    down_other_end = across(down_end)
    cot_end.append(inward(after(cotangent[:, cuts[1]], down_end, down_other)))
    cot_other_end = [across(cot_end[0])]
    up_end = inward(after(up, tokens_end, cot_end[0]))
    down_there = [outward(down), outward(down_other), outward(down_other_end)]

    tokens_mine = jnp.concatenate([tokens, after(tokens_end, down_there[0])], axis=0)
    down_all = jnp.concatenate([down, down_end, down_other, down_other_end], axis=0)
    down_used = jnp.where(
        middle,
        down_all,
        jnp.concatenate([down_there[0], down, down_there[1], down_there[2]], axis=0),
    )

    latent = col_sum(rows_dot(tokens_mine, down_all))
    inv_rms = lax.rsqrt(jnp.mean(latent * latent, axis=-1, keepdims=True) + 1e-06)
    normed = latent * inv_rms
    normed_bf = normed.astype(BF16)
    normed_sent = after(normed_bf[:, 2 * lat :], down_there[1])
    normed_other = across(normed_sent)
    normed_all = jnp.concatenate([normed_bf[:, : 2 * lat], normed_other], axis=0)

    cot_other_end.append(across(after(cot_end[1], normed_sent)))
    def early_rows(k):
        return jnp.concatenate([cotangent[:, cuts[k]], cot_end[k], cot_other[:, cuts[k]]], axis=0)

    values = jnp.concatenate([early_rows(0), cot_other_end[0]], axis=0)
    up_first = tokens_dot(after(normed_all, down_there[2]), values).astype(BF16)
    back_first = outward(up_first[lat:])
    up_mine = jnp.concatenate([up, after(up_end, up_first, down_used)], axis=0)
    grad = rows_dot(values, up_mine[:, cuts[0]])
    early = grad[: 3 * rows] + rows_dot(early_rows(1), up_mine[:, cuts[1]])
    early = early.astype(BF16)
    early_sum = early.astype(F32) + other_col(early).astype(F32)

    last = after(cot_other_end[1], early)
    late = col_sum(grad[3 * rows :] + rows_dot(last, up_mine[:, cuts[1]]))
    values = jnp.concatenate([early_rows(1), last], axis=0)
    up_second = tokens_dot(normed_all, values).astype(BF16)
    back_second = outward(up_second[lat:])
    grad_sent = jnp.concatenate([early_sum[2 * rows :], late], axis=0).astype(BF16)
    from_across = across(after(grad_sent, up_second, back_first))
    normed_grad = jnp.concatenate([early_sum[: 2 * rows], from_across.astype(F32)], axis=1)
    inner = jnp.mean(normed_grad * normed, axis=-1, keepdims=True)
    latent_bf = (inv_rms * (normed_grad - normed * inner)).astype(BF16)
    latent_there = outward(latent_bf[rows:])
    latent_used = jnp.where(middle, latent_bf[:rows], latent_there)

    sums = [
        tokens_dot(latent_bf[:, j * lat : (j + 1) * lat], tokens_mine).astype(BF16)
        for j in range(4)
    ]
    width = tokens.shape[1] // 2
    halves = (slice(0, width), slice(width, 2 * width))
    sent_end, sent_own = sums[3], sums[2]
    from_end = [across(sent_end[:, half]) for half in halves]
    end_first = (sums[1][:, halves[0]] + from_end[0].astype(F32)).astype(BF16)
    from_own = across(after(sent_own, end_first))
    end_second = sums[1][:, halves[1]] + after(from_end[1], end_first).astype(F32)
    end_second = end_second.astype(BF16)
    down_end_grad = jnp.concatenate([outward(end_first), outward(end_second)], axis=1)
    up_grad = jnp.concatenate(
        [
            jnp.where(middle, up_first[:lat], back_first),
            jnp.where(middle, up_second[:lat], after(back_second, end_second)),
        ],
        axis=1,
    )

    input_grad = jnp.dot(latent_used, down_used, preferred_element_type=F32).astype(BF16)
    passed = shifted(input_grad, "section", -1)
    down_own_grad = (sums[0] + after(from_own, passed).astype(F32)).astype(BF16)
    down_grad = jnp.where(middle, down_own_grad, down_end_grad)
    return (passed[None], down_grad[None], up_grad[None])


def solution(mesh):
    spec = P("section", "row", "col")
    folds = mesh.shape["row"] == 4 and mesh.shape["col"] == 2
    return jax.shard_map(
        folded_body if folds else general_body,
        mesh=mesh,
        in_specs=(spec,) * 4,
        out_specs=(spec,) * 3,
        check_vma=False,
    )
```

```python
import jax
import jax.numpy as jnp
from jax import lax
from jax.sharding import PartitionSpec as P

F32 = jnp.float32
BF16 = jnp.bfloat16


def shifted(value, axis, steps):
    count = lax.axis_size(axis)
    leading, last = (max(0, -steps), min(count, count - steps))
    return lax.ppermute(value, axis, [(source, source + steps) for source in range(leading, last)])


def general_body(inputs, down_weight, up_weight, value_grad):
    tokens = inputs[0]
    cotangent = value_grad[0]
    down_full = lax.all_gather(down_weight[0], "row", axis=0, tiled=True)
    up_full = lax.all_gather(up_weight[0], "row", axis=0, tiled=True)
    latent_part = jnp.einsum("td,ld->tl", tokens, down_full, preferred_element_type=F32)
    grad_part = jnp.einsum("tf,lf->tl", cotangent, up_full, preferred_element_type=F32)
    latent = lax.psum(latent_part.astype(BF16), "col").astype(F32)
    normed_grad = lax.psum(grad_part.astype(BF16), "col").astype(F32)
    inv_rms = lax.rsqrt(jnp.mean(latent * latent, axis=-1, keepdims=True) + 1e-06)
    normed = latent * inv_rms
    normed_bf = normed.astype(BF16)
    inner = jnp.mean(normed_grad * normed, axis=-1, keepdims=True)
    latent_bf = (inv_rms * (normed_grad - normed * inner)).astype(BF16)
    up_grad = lax.psum_scatter(
        jnp.einsum("tl,tf->lf", normed_bf, cotangent, preferred_element_type=F32).astype(BF16),
        "row",
        scatter_dimension=0,
        tiled=True,
    )
    down_grad = lax.psum_scatter(
        jnp.einsum("tl,td->ld", latent_bf, tokens, preferred_element_type=F32).astype(BF16),
        "row",
        scatter_dimension=0,
        tiled=True,
    )
    input_grad = jnp.einsum("tl,ld->td", latent_bf, down_full, preferred_element_type=F32)
    passed = shifted(input_grad.astype(BF16), "section", -1)
    return (passed[None], down_grad[None], up_grad[None])


def inward(value):
    return lax.ppermute(value, "row", [(0, 1), (3, 2)])


def across(value):
    return lax.ppermute(value, "row", [(1, 2), (2, 1)])


def outward(value):
    return lax.ppermute(value, "row", [(1, 0), (2, 3)])


def other_col(value):
    return lax.ppermute(value, "col", [(0, 1), (1, 0)])


def after(value, *earlier):
    return lax.optimization_barrier((value, *earlier))[0]


def rows_dot(left, right):
    return lax.dot_general(left, right, (((1,), (1,)), ((), ())), preferred_element_type=F32)


def tokens_dot(left, right):
    return lax.dot_general(left, right, (((0,), (0,)), ((), ())), preferred_element_type=F32)


def col_sum(part):
    sent = part.astype(BF16)
    return sent.astype(F32) + other_col(sent).astype(F32)


def folded_body(inputs, down_weight, up_weight, value_grad):
    tokens, down, up, cotangent = inputs[0], down_weight[0], up_weight[0], value_grad[0]
    rows = tokens.shape[0]
    lat = down.shape[0]
    feat = cotangent.shape[1]
    place = lax.axis_index("row")
    middle = (place == 1) | (place == 2)

    cut = feat // 2
    cuts = (slice(0, cut), slice(cut, feat))
    down_end = inward(down)
    tokens_end = inward(tokens)
    down_other = across(down)
    cot_other = across(cotangent)
    cot_end = [inward(cotangent[:, cuts[0]])]
    down_other_end = across(down_end)
    cot_end.append(inward(after(cotangent[:, cuts[1]], down_end, down_other)))
    cot_other_end = [across(cot_end[0])]
    up_end = inward(after(up, tokens_end, cot_end[0]))
    down_there = [outward(down), outward(down_other), outward(down_other_end)]

    tokens_mine = jnp.concatenate([tokens, after(tokens_end, down_there[0])], axis=0)
    down_all = jnp.concatenate([down, down_end, down_other, down_other_end], axis=0)
    down_used = jnp.where(
        middle,
        down_all,
        jnp.concatenate([down_there[0], down, down_there[1], down_there[2]], axis=0),
    )

    latent = col_sum(rows_dot(tokens_mine, down_all))
    inv_rms = lax.rsqrt(jnp.mean(latent * latent, axis=-1, keepdims=True) + 1e-06)
    normed = latent * inv_rms
    normed_bf = normed.astype(BF16)
    normed_sent = after(normed_bf[:, 2 * lat :], down_there[1])
    normed_other = across(normed_sent)
    normed_all = jnp.concatenate([normed_bf[:, : 2 * lat], normed_other], axis=0)

    cot_other_end.append(across(after(cot_end[1], normed_sent)))
    def early_rows(k):
        return jnp.concatenate([cotangent[:, cuts[k]], cot_end[k], cot_other[:, cuts[k]]], axis=0)

    values = jnp.concatenate([early_rows(0), cot_other_end[0]], axis=0)
    up_first = tokens_dot(after(normed_all, down_there[2]), values).astype(BF16)
    back_first = outward(up_first[lat:])
    up_mine = jnp.concatenate([up, after(up_end, up_first, down_used)], axis=0)
    grad = rows_dot(values, up_mine[:, cuts[0]])
    early = grad[: 3 * rows] + rows_dot(early_rows(1), up_mine[:, cuts[1]])
    early = early.astype(BF16)
    early_sum = early.astype(F32) + other_col(early).astype(F32)

    last = after(cot_other_end[1], early)
    late = col_sum(grad[3 * rows :] + rows_dot(last, up_mine[:, cuts[1]]))
    values = jnp.concatenate([early_rows(1), last], axis=0)
    up_second = tokens_dot(normed_all, values).astype(BF16)
    back_second = outward(up_second[lat:])
    grad_sent = jnp.concatenate([early_sum[2 * rows :], late], axis=0).astype(BF16)
    from_across = across(after(grad_sent, up_second, back_first))
    normed_grad = jnp.concatenate([early_sum[: 2 * rows], from_across.astype(F32)], axis=1)
    inner = jnp.mean(normed_grad * normed, axis=-1, keepdims=True)
    latent_bf = (inv_rms * (normed_grad - normed * inner)).astype(BF16)

    sums = [
        tokens_dot(latent_bf[:, j * lat : (j + 1) * lat], tokens_mine).astype(BF16)
        for j in range(4)
    ]
    width = tokens.shape[1] // 2
    halves = (slice(0, width), slice(width, 2 * width))
    sent_end, sent_own = sums[3], sums[2]
    from_end = [across(sent_end[:, half]) for half in halves]
    end_first = (sums[1][:, halves[0]] + from_end[0].astype(F32)).astype(BF16)
    from_own = across(after(sent_own, end_first))
    end_second = sums[1][:, halves[1]] + after(from_end[1], end_first).astype(F32)
    end_second = end_second.astype(BF16)
    down_end_grad = jnp.concatenate([outward(end_first), outward(end_second)], axis=1)
    up_grad = jnp.concatenate(
        [
            jnp.where(middle, up_first[:lat], back_first),
            jnp.where(middle, up_second[:lat], after(back_second, end_second)),
        ],
        axis=1,
    )

    latent_there = outward(latent_bf[rows:])
    latent_used = jnp.where(middle, latent_bf[:rows], after(latent_there, end_first))
    input_grad = jnp.dot(latent_used, down_used, preferred_element_type=F32).astype(BF16)
    passed = shifted(input_grad[None], "section", -1)
    down_own_grad = (sums[0] + after(from_own, passed).astype(F32)).astype(BF16)
    down_grad = jnp.where(middle, down_own_grad, down_end_grad)
    return (passed, down_grad[None], up_grad[None])


def solution(mesh):
    spec = P("section", "row", "col")
    folds = mesh.shape["row"] == 4 and mesh.shape["col"] == 2
    return jax.shard_map(
        folded_body if folds else general_body,
        mesh=mesh,
        in_specs=(spec,) * 4,
        out_specs=(spec,) * 3,
        check_vma=False,
    )
```

```python
import jax
import jax.numpy as jnp
from jax import lax
from jax.sharding import PartitionSpec as P

F32 = jnp.float32
BF16 = jnp.bfloat16


def shifted(value, axis, steps):
    count = lax.axis_size(axis)
    leading, last = (max(0, -steps), min(count, count - steps))
    return lax.ppermute(value, axis, [(source, source + steps) for source in range(leading, last)])


def general_body(inputs, down_weight, up_weight, value_grad):
    tokens = inputs[0]
    cotangent = value_grad[0]
    down_full = lax.all_gather(down_weight[0], "row", axis=0, tiled=True)
    up_full = lax.all_gather(up_weight[0], "row", axis=0, tiled=True)
    latent_part = jnp.einsum("td,ld->tl", tokens, down_full, preferred_element_type=F32)
    grad_part = jnp.einsum("tf,lf->tl", cotangent, up_full, preferred_element_type=F32)
    latent = lax.psum(latent_part.astype(BF16), "col").astype(F32)
    normed_grad = lax.psum(grad_part.astype(BF16), "col").astype(F32)
    inv_rms = lax.rsqrt(jnp.mean(latent * latent, axis=-1, keepdims=True) + 1e-06)
    normed = latent * inv_rms
    normed_bf = normed.astype(BF16)
    inner = jnp.mean(normed_grad * normed, axis=-1, keepdims=True)
    latent_bf = (inv_rms * (normed_grad - normed * inner)).astype(BF16)
    up_grad = lax.psum_scatter(
        jnp.einsum("tl,tf->lf", normed_bf, cotangent, preferred_element_type=F32).astype(BF16),
        "row",
        scatter_dimension=0,
        tiled=True,
    )
    down_grad = lax.psum_scatter(
        jnp.einsum("tl,td->ld", latent_bf, tokens, preferred_element_type=F32).astype(BF16),
        "row",
        scatter_dimension=0,
        tiled=True,
    )
    input_grad = jnp.einsum("tl,ld->td", latent_bf, down_full, preferred_element_type=F32)
    passed = shifted(input_grad.astype(BF16), "section", -1)
    return (passed[None], down_grad[None], up_grad[None])


def inward(value):
    return lax.ppermute(value, "row", [(0, 1), (3, 2)])


def across(value):
    return lax.ppermute(value, "row", [(1, 2), (2, 1)])


def outward(value):
    return lax.ppermute(value, "row", [(1, 0), (2, 3)])


def other_col(value):
    return lax.ppermute(value, "col", [(0, 1), (1, 0)])


def after(value, *earlier):
    return lax.optimization_barrier((value, *earlier))[0]


def rows_dot(left, right):
    return lax.dot_general(left, right, (((1,), (1,)), ((), ())), preferred_element_type=F32)


def tokens_dot(left, right):
    return lax.dot_general(left, right, (((0,), (0,)), ((), ())), preferred_element_type=F32)


def col_sum(part):
    sent = part.astype(BF16)
    return sent.astype(F32) + other_col(sent).astype(F32)


def folded_body(inputs, down_weight, up_weight, value_grad):
    tokens, down, up, cotangent = inputs[0], down_weight[0], up_weight[0], value_grad[0]
    rows = tokens.shape[0]
    lat = down.shape[0]
    feat = cotangent.shape[1]
    place = lax.axis_index("row")
    middle = (place == 1) | (place == 2)

    cut = feat // 2
    cuts = (slice(0, cut), slice(cut, feat))
    down_end = inward(down)
    tokens_end = inward(tokens)
    down_other = across(down)
    cot_other = across(cotangent)
    cot_end = [inward(cotangent[:, cuts[0]])]
    down_other_end = across(down_end)
    cot_end.append(inward(after(cotangent[:, cuts[1]], down_end, down_other)))
    cot_other_end = [across(cot_end[0])]
    up_end = inward(after(up, tokens_end, cot_end[0]))
    down_there = [outward(down), outward(down_other), outward(down_other_end)]

    tokens_mine = jnp.concatenate([tokens, after(tokens_end, down_there[0])], axis=0)
    down_all = jnp.concatenate([down, down_end, down_other, down_other_end], axis=0)
    down_used = jnp.where(
        middle,
        down_all,
        jnp.concatenate([down_there[0], down, down_there[1], down_there[2]], axis=0),
    )

    latent = col_sum(rows_dot(tokens_mine, down_all))
    inv_rms = lax.rsqrt(jnp.mean(latent * latent, axis=-1, keepdims=True) + 1e-06)
    normed = latent * inv_rms
    normed_bf = normed.astype(BF16)
    normed_sent = after(normed_bf[:, 2 * lat :], down_there[1])
    normed_other = across(normed_sent)
    normed_all = jnp.concatenate([normed_bf[:, : 2 * lat], normed_other], axis=0)

    cot_other_end.append(across(after(cot_end[1], normed_sent)))
    def early_rows(k):
        return jnp.concatenate([cotangent[:, cuts[k]], cot_end[k], cot_other[:, cuts[k]]], axis=0)

    values = jnp.concatenate([early_rows(0), cot_other_end[0]], axis=0)
    up_first = tokens_dot(after(normed_all, down_there[2]), values).astype(BF16)
    back_first = outward(up_first[lat:])
    up_mine = jnp.concatenate([up, after(up_end, up_first, down_used)], axis=0)
    grad = rows_dot(values, up_mine[:, cuts[0]])
    early = grad[: 3 * rows] + rows_dot(early_rows(1), up_mine[:, cuts[1]])
    early = early.astype(BF16)
    early_sum = early.astype(F32) + other_col(early).astype(F32)

    last = after(cot_other_end[1], early)
    late = col_sum(grad[3 * rows :] + rows_dot(last, up_mine[:, cuts[1]]))
    values = jnp.concatenate([early_rows(1), last], axis=0)
    up_second = tokens_dot(normed_all, values).astype(BF16)
    back_second = outward(up_second[lat:])
    grad_sent = jnp.concatenate([early_sum[2 * rows :], late], axis=0).astype(BF16)
    from_across = across(after(grad_sent, up_second, back_first))
    normed_grad = jnp.concatenate([early_sum[: 2 * rows], from_across.astype(F32)], axis=1)
    inner = jnp.mean(normed_grad * normed, axis=-1, keepdims=True)
    latent_bf = (inv_rms * (normed_grad - normed * inner)).astype(BF16)

    sums = [
        tokens_dot(latent_bf[:, j * lat : (j + 1) * lat], tokens_mine).astype(BF16)
        for j in range(3)
    ]
    width = tokens.shape[1] // 2
    halves = (slice(0, width), slice(width, 2 * width))
    sent_own = sums[2]
    sent_halves = [tokens_dot(latent_bf[:, 3 * lat :], tokens_mine[:, half]).astype(BF16) for half in halves]
    from_end = [across(half) for half in sent_halves]
    end_first = (sums[1][:, halves[0]] + from_end[0].astype(F32)).astype(BF16)
    from_own = across(after(sent_own, end_first))
    end_second = sums[1][:, halves[1]] + after(from_end[1], end_first).astype(F32)
    end_second = end_second.astype(BF16)
    down_end_grad = jnp.concatenate([outward(end_first), outward(end_second)], axis=1)
    up_grad = jnp.concatenate(
        [
            jnp.where(middle, up_first[:lat], back_first),
            jnp.where(middle, up_second[:lat], after(back_second, end_second)),
        ],
        axis=1,
    )

    latent_there = outward(after(latent_bf[rows:], *sent_halves))
    latent_used = jnp.where(middle, latent_bf[:rows], latent_there)
    input_grad = jnp.dot(latent_used, down_used, preferred_element_type=F32).astype(BF16)
    passed = shifted(input_grad, "section", -1)
    final = lax.axis_index("section") == lax.axis_size("section") - 1
    passed = jnp.where(final, jnp.zeros_like(passed), passed)
    down_own_grad = (sums[0] + after(from_own, passed).astype(F32)).astype(BF16)
    down_grad = jnp.where(middle, down_own_grad, down_end_grad)
    return (passed[None], down_grad[None], up_grad[None])


def solution(mesh):
    spec = P("section", "row", "col")
    folds = mesh.shape["row"] == 4 and mesh.shape["col"] == 2
    return jax.shard_map(
        folded_body if folds else general_body,
        mesh=mesh,
        in_specs=(spec,) * 4,
        out_specs=(spec,) * 3,
        check_vma=False,
    )
```

```python
import jax
import jax.numpy as jnp
from jax import lax
from jax.sharding import PartitionSpec as P

F32 = jnp.float32
BF16 = jnp.bfloat16


def shifted(value, axis, steps):
    count = lax.axis_size(axis)
    leading, last = (max(0, -steps), min(count, count - steps))
    return lax.ppermute(value, axis, [(source, source + steps) for source in range(leading, last)])


def general_body(inputs, down_weight, up_weight, value_grad):
    tokens = inputs[0]
    cotangent = value_grad[0]
    down_full = lax.all_gather(down_weight[0], "row", axis=0, tiled=True)
    up_full = lax.all_gather(up_weight[0], "row", axis=0, tiled=True)
    latent_part = jnp.einsum("td,ld->tl", tokens, down_full, preferred_element_type=F32)
    grad_part = jnp.einsum("tf,lf->tl", cotangent, up_full, preferred_element_type=F32)
    latent = lax.psum(latent_part.astype(BF16), "col").astype(F32)
    normed_grad = lax.psum(grad_part.astype(BF16), "col").astype(F32)
    inv_rms = lax.rsqrt(jnp.mean(latent * latent, axis=-1, keepdims=True) + 1e-06)
    normed = latent * inv_rms
    normed_bf = normed.astype(BF16)
    inner = jnp.mean(normed_grad * normed, axis=-1, keepdims=True)
    latent_bf = (inv_rms * (normed_grad - normed * inner)).astype(BF16)
    up_grad = lax.psum_scatter(
        jnp.einsum("tl,tf->lf", normed_bf, cotangent, preferred_element_type=F32).astype(BF16),
        "row",
        scatter_dimension=0,
        tiled=True,
    )
    down_grad = lax.psum_scatter(
        jnp.einsum("tl,td->ld", latent_bf, tokens, preferred_element_type=F32).astype(BF16),
        "row",
        scatter_dimension=0,
        tiled=True,
    )
    input_grad = jnp.einsum("tl,ld->td", latent_bf, down_full, preferred_element_type=F32)
    passed = shifted(input_grad.astype(BF16), "section", -1)
    return (passed[None], down_grad[None], up_grad[None])


def inward(value):
    return lax.ppermute(value, "row", [(0, 1), (3, 2)])


def across(value):
    return lax.ppermute(value, "row", [(1, 2), (2, 1)])


def outward(value):
    return lax.ppermute(value, "row", [(1, 0), (2, 3)])


def other_col(value):
    return lax.ppermute(value, "col", [(0, 1), (1, 0)])


def after(value, *earlier):
    return lax.optimization_barrier((value, *earlier))[0]


def rows_dot(left, right):
    return lax.dot_general(left, right, (((1,), (1,)), ((), ())), preferred_element_type=F32)


def tokens_dot(left, right):
    return lax.dot_general(left, right, (((0,), (0,)), ((), ())), preferred_element_type=F32)


def col_sum(part):
    sent = part.astype(BF16)
    return sent.astype(F32) + other_col(sent).astype(F32)


def folded_body(inputs, down_weight, up_weight, value_grad):
    tokens, down, up, cotangent = inputs[0], down_weight[0], up_weight[0], value_grad[0]
    rows = tokens.shape[0]
    lat = down.shape[0]
    feat = cotangent.shape[1]
    place = lax.axis_index("row")
    middle = (place == 1) | (place == 2)

    cut = feat // 2
    cuts = (slice(0, cut), slice(cut, feat))
    down_end = inward(down)
    tokens_end = inward(tokens)
    down_other = across(down)
    cot_other = across(cotangent)
    cot_end = [inward(cotangent[:, cuts[0]])]
    down_other_end = across(down_end)
    cot_end.append(inward(after(cotangent[:, cuts[1]], down_end, down_other)))
    cot_other_end = [across(cot_end[0])]
    up_end = inward(after(up, tokens_end, cot_end[0]))
    down_there = [outward(down), outward(down_other), outward(down_other_end)]

    tokens_mine = jnp.concatenate([tokens, after(tokens_end, down_there[0])], axis=0)
    down_all = jnp.concatenate([down, down_end, down_other, down_other_end], axis=0)
    down_used = jnp.where(
        middle,
        down_all,
        jnp.concatenate([down_there[0], down, down_there[1], down_there[2]], axis=0),
    )

    latent = col_sum(rows_dot(tokens_mine, down_all))
    inv_rms = lax.rsqrt(jnp.mean(latent * latent, axis=-1, keepdims=True) + 1e-06)
    normed = latent * inv_rms
    normed_bf = normed.astype(BF16)
    normed_sent = after(normed_bf[:, 2 * lat :], down_there[1])
    normed_other = across(normed_sent)
    normed_all = jnp.concatenate([normed_bf[:, : 2 * lat], normed_other], axis=0)

    cot_other_end.append(across(after(cot_end[1], normed_sent)))
    def early_rows(k):
        return jnp.concatenate([cotangent[:, cuts[k]], cot_end[k], cot_other[:, cuts[k]]], axis=0)

    values = jnp.concatenate([early_rows(0), cot_other_end[0]], axis=0)
    up_first = tokens_dot(after(normed_all, down_there[2]), values).astype(BF16)
    back_first = outward(up_first[lat:])
    up_mine = jnp.concatenate([up, after(up_end, up_first, down_used)], axis=0)
    grad = rows_dot(values, up_mine[:, cuts[0]])
    early = grad[: 3 * rows] + rows_dot(early_rows(1), up_mine[:, cuts[1]])
    early = early.astype(BF16)
    early_sum = early.astype(F32) + other_col(early).astype(F32)

    last = after(cot_other_end[1], early)
    late = col_sum(grad[3 * rows :] + rows_dot(last, up_mine[:, cuts[1]]))
    values = jnp.concatenate([early_rows(1), last], axis=0)
    up_second = tokens_dot(normed_all, values).astype(BF16)
    back_second = outward(up_second[lat:])
    grad_sent = jnp.concatenate([early_sum[2 * rows :], late], axis=0).astype(BF16)
    from_across = across(after(grad_sent, up_second, back_first))
    normed_grad = jnp.concatenate([early_sum[: 2 * rows], from_across.astype(F32)], axis=1)
    inner = jnp.mean(normed_grad * normed, axis=-1, keepdims=True)
    latent_bf = (inv_rms * (normed_grad - normed * inner)).astype(BF16)

    sums = [
        tokens_dot(latent_bf[:, j * lat : (j + 1) * lat], tokens_mine).astype(BF16)
        for j in range(3)
    ]
    width = tokens.shape[1] // 2
    halves = (slice(0, width), slice(width, 2 * width))
    sent_own = sums[2]
    sent_halves = [tokens_dot(latent_bf[:, 3 * lat :], tokens_mine[:, half]).astype(BF16) for half in halves]
    from_end = [across(half) for half in sent_halves]
    end_first = (sums[1][:, halves[0]] + from_end[0].astype(F32)).astype(BF16)
    from_own = across(after(sent_own, end_first))
    end_second = sums[1][:, halves[1]] + after(from_end[1], end_first).astype(F32)
    end_second = end_second.astype(BF16)
    down_end_grad = jnp.concatenate([outward(end_first), outward(end_second)], axis=1)
    up_grad = jnp.concatenate(
        [
            jnp.where(middle, up_first[:lat], back_first),
            jnp.where(middle, up_second[:lat], after(back_second, end_second)),
        ],
        axis=1,
    )

    latent_there = outward(after(latent_bf[rows:], *sent_halves))
    latent_used = jnp.where(middle, latent_bf[:rows], latent_there)
    input_grad = jnp.dot(latent_used, down_used, preferred_element_type=F32).astype(BF16)
    passed = shifted(input_grad, "section", -1)
    down_own_grad = (sums[0] + after(from_own, passed).astype(F32)).astype(BF16)
    down_grad = jnp.where(middle, down_own_grad, down_end_grad)
    return (passed[None], down_grad[None], up_grad[None])


def solution(mesh):
    spec = P("section", "row", "col")
    folds = mesh.shape["row"] == 4 and mesh.shape["col"] == 2
    return jax.shard_map(
        folded_body if folds else general_body,
        mesh=mesh,
        in_specs=(spec,) * 4,
        out_specs=(spec,) * 3,
        check_vma=False,
    )
```

```python
import jax
import jax.numpy as jnp
from jax import lax
from jax.sharding import PartitionSpec as P

F32 = jnp.float32
BF16 = jnp.bfloat16


def shifted(value, axis, steps):
    count = lax.axis_size(axis)
    leading, last = (max(0, -steps), min(count, count - steps))
    return lax.ppermute(value, axis, [(source, source + steps) for source in range(leading, last)])


def general_body(inputs, down_weight, up_weight, value_grad):
    tokens = inputs[0]
    cotangent = value_grad[0]
    down_full = lax.all_gather(down_weight[0], "row", axis=0, tiled=True)
    up_full = lax.all_gather(up_weight[0], "row", axis=0, tiled=True)
    latent_part = jnp.einsum("td,ld->tl", tokens, down_full, preferred_element_type=F32)
    grad_part = jnp.einsum("tf,lf->tl", cotangent, up_full, preferred_element_type=F32)
    latent = lax.psum(latent_part.astype(BF16), "col").astype(F32)
    normed_grad = lax.psum(grad_part.astype(BF16), "col").astype(F32)
    inv_rms = lax.rsqrt(jnp.mean(latent * latent, axis=-1, keepdims=True) + 1e-06)
    normed = latent * inv_rms
    normed_bf = normed.astype(BF16)
    inner = jnp.mean(normed_grad * normed, axis=-1, keepdims=True)
    latent_bf = (inv_rms * (normed_grad - normed * inner)).astype(BF16)
    up_grad = lax.psum_scatter(
        jnp.einsum("tl,tf->lf", normed_bf, cotangent, preferred_element_type=F32).astype(BF16),
        "row",
        scatter_dimension=0,
        tiled=True,
    )
    down_grad = lax.psum_scatter(
        jnp.einsum("tl,td->ld", latent_bf, tokens, preferred_element_type=F32).astype(BF16),
        "row",
        scatter_dimension=0,
        tiled=True,
    )
    input_grad = jnp.einsum("tl,ld->td", latent_bf, down_full, preferred_element_type=F32)
    passed = shifted(input_grad.astype(BF16), "section", -1)
    return (passed[None], down_grad[None], up_grad[None])


def inward(value):
    return lax.ppermute(value, "row", [(0, 1), (3, 2)])


def across(value):
    return lax.ppermute(value, "row", [(1, 2), (2, 1)])


def outward(value):
    return lax.ppermute(value, "row", [(1, 0), (2, 3)])


def other_col(value):
    return lax.ppermute(value, "col", [(0, 1), (1, 0)])


def after(value, *earlier):
    return lax.optimization_barrier((value, *earlier))[0]


def rows_dot(left, right):
    return lax.dot_general(left, right, (((1,), (1,)), ((), ())), preferred_element_type=F32)


def tokens_dot(left, right):
    return lax.dot_general(left, right, (((0,), (0,)), ((), ())), preferred_element_type=F32)


def col_sum(part):
    sent = part.astype(BF16)
    return sent.astype(F32) + other_col(sent).astype(F32)


def folded_body(inputs, down_weight, up_weight, value_grad):
    tokens, down, up, cotangent = inputs[0], down_weight[0], up_weight[0], value_grad[0]
    rows = tokens.shape[0]
    lat = down.shape[0]
    feat = cotangent.shape[1]
    place = lax.axis_index("row")
    middle = (place == 1) | (place == 2)

    cut = feat // 2
    cuts = (slice(0, cut), slice(cut, feat))
    down_end = inward(down)
    tokens_end = inward(tokens)
    down_other = across(down)
    cot_other = across(cotangent)
    cot_end = [inward(cotangent[:, cuts[0]])]
    down_other_end = across(down_end)
    cot_end.append(inward(after(cotangent[:, cuts[1]], down_end, down_other)))
    cot_other_end = [across(cot_end[0])]
    up_end = inward(after(up, tokens_end, cot_end[0]))
    down_there = [outward(down), outward(down_other), outward(down_other_end)]

    tokens_mine = jnp.concatenate([tokens, after(tokens_end, down_there[0])], axis=0)
    down_all = jnp.concatenate([down, down_end, down_other, down_other_end], axis=0)
    down_used = jnp.where(
        middle,
        down_all,
        jnp.concatenate([down_there[0], down, down_there[1], down_there[2]], axis=0),
    )

    latent = col_sum(rows_dot(tokens_mine, down_all))
    inv_rms = lax.rsqrt(jnp.mean(latent * latent, axis=-1, keepdims=True) + 1e-06)
    normed = latent * inv_rms
    normed_bf = normed.astype(BF16)
    normed_sent = after(normed_bf[:, 2 * lat :], down_there[1])
    normed_other = across(normed_sent)
    normed_all = jnp.concatenate([normed_bf[:, : 2 * lat], normed_other], axis=0)

    cot_other_end.append(across(after(cot_end[1], normed_sent)))
    def early_rows(k):
        return jnp.concatenate([cotangent[:, cuts[k]], cot_end[k], cot_other[:, cuts[k]]], axis=0)

    values = jnp.concatenate([early_rows(0), cot_other_end[0]], axis=0)
    up_first = tokens_dot(after(normed_all, down_there[2]), values).astype(BF16)
    back_first = outward(up_first[lat:])
    up_mine = jnp.concatenate([up, after(up_end, up_first, down_used)], axis=0)
    grad = rows_dot(values, up_mine[:, cuts[0]])
    early = grad[: 3 * rows] + rows_dot(early_rows(1), up_mine[:, cuts[1]])
    early = early.astype(BF16)
    early_sum = early.astype(F32) + other_col(early).astype(F32)

    last = after(cot_other_end[1], early)
    late = col_sum(grad[3 * rows :] + rows_dot(last, up_mine[:, cuts[1]]))
    values = jnp.concatenate([early_rows(1), last], axis=0)
    up_second = tokens_dot(normed_all, values).astype(BF16)
    back_second = outward(up_second[lat:])
    grad_sent = jnp.concatenate([early_sum[2 * rows :], late], axis=0).astype(BF16)
    from_across = across(after(grad_sent, up_second, back_first))
    normed_grad = jnp.concatenate([early_sum[: 2 * rows], from_across.astype(F32)], axis=1)
    inner = jnp.mean(normed_grad * normed, axis=-1, keepdims=True)
    latent_bf = (inv_rms * (normed_grad - normed * inner)).astype(BF16)
    latent_there = outward(latent_bf[rows:])
    latent_used = jnp.where(middle, latent_bf[:rows], latent_there)

    sums = [
        tokens_dot(latent_bf[:, j * lat : (j + 1) * lat], tokens_mine).astype(BF16)
        for j in range(4)
    ]
    width = tokens.shape[1] // 2
    halves = (slice(0, width), slice(width, 2 * width))
    sent_end, sent_own = sums[3], sums[2]
    from_end = [across(sent_end[:, half]) for half in halves]
    end_first = (sums[1][:, halves[0]] + from_end[0].astype(F32)).astype(BF16)
    from_own = across(after(sent_own, latent_there))
    end_second = sums[1][:, halves[1]] + after(from_end[1], end_first).astype(F32)
    end_second = end_second.astype(BF16)
    down_end_grad = jnp.concatenate([outward(end_first), outward(end_second)], axis=1)
    up_grad = jnp.concatenate(
        [
            jnp.where(middle, up_first[:lat], back_first),
            jnp.where(middle, up_second[:lat], after(back_second, end_second)),
        ],
        axis=1,
    )

    input_grad = jnp.dot(latent_used, down_used, preferred_element_type=F32).astype(BF16)
    passed = shifted(input_grad, "section", -1)
    down_own_grad = (sums[0] + after(from_own, passed).astype(F32)).astype(BF16)
    down_grad = jnp.where(middle, down_own_grad, down_end_grad)
    return (passed[None], down_grad[None], up_grad[None])


def solution(mesh):
    spec = P("section", "row", "col")
    folds = mesh.shape["row"] == 4 and mesh.shape["col"] == 2
    return jax.shard_map(
        folded_body if folds else general_body,
        mesh=mesh,
        in_specs=(spec,) * 4,
        out_specs=(spec,) * 3,
        check_vma=False,
    )
```

```python
import jax
import jax.numpy as jnp
from jax import lax
from jax.sharding import PartitionSpec as P

F32 = jnp.float32
BF16 = jnp.bfloat16


def shifted(value, axis, steps):
    count = lax.axis_size(axis)
    leading, last = (max(0, -steps), min(count, count - steps))
    return lax.ppermute(value, axis, [(source, source + steps) for source in range(leading, last)])


def general_body(inputs, down_weight, up_weight, value_grad):
    tokens = inputs[0]
    cotangent = value_grad[0]
    down_full = lax.all_gather(down_weight[0], "row", axis=0, tiled=True)
    up_full = lax.all_gather(up_weight[0], "row", axis=0, tiled=True)
    latent_part = jnp.einsum("td,ld->tl", tokens, down_full, preferred_element_type=F32)
    grad_part = jnp.einsum("tf,lf->tl", cotangent, up_full, preferred_element_type=F32)
    latent = lax.psum(latent_part.astype(BF16), "col").astype(F32)
    normed_grad = lax.psum(grad_part.astype(BF16), "col").astype(F32)
    inv_rms = lax.rsqrt(jnp.mean(latent * latent, axis=-1, keepdims=True) + 1e-06)
    normed = latent * inv_rms
    normed_bf = normed.astype(BF16)
    inner = jnp.mean(normed_grad * normed, axis=-1, keepdims=True)
    latent_bf = (inv_rms * (normed_grad - normed * inner)).astype(BF16)
    up_grad = lax.psum_scatter(
        jnp.einsum("tl,tf->lf", normed_bf, cotangent, preferred_element_type=F32).astype(BF16),
        "row",
        scatter_dimension=0,
        tiled=True,
    )
    down_grad = lax.psum_scatter(
        jnp.einsum("tl,td->ld", latent_bf, tokens, preferred_element_type=F32).astype(BF16),
        "row",
        scatter_dimension=0,
        tiled=True,
    )
    input_grad = jnp.einsum("tl,ld->td", latent_bf, down_full, preferred_element_type=F32)
    passed = shifted(input_grad.astype(BF16), "section", -1)
    return (passed[None], down_grad[None], up_grad[None])


def inward(value):
    return lax.ppermute(value, "row", [(0, 1), (3, 2)])


def across(value):
    return lax.ppermute(value, "row", [(1, 2), (2, 1)])


def outward(value):
    return lax.ppermute(value, "row", [(1, 0), (2, 3)])


def other_col(value):
    return lax.ppermute(value, "col", [(0, 1), (1, 0)])


def after(value, *earlier):
    return lax.optimization_barrier((value, *earlier))[0]


def rows_dot(left, right):
    return lax.dot_general(left, right, (((1,), (1,)), ((), ())), preferred_element_type=F32)


def tokens_dot(left, right):
    return lax.dot_general(left, right, (((0,), (0,)), ((), ())), preferred_element_type=F32)


def col_sum(part):
    sent = part.astype(BF16)
    return sent.astype(F32) + other_col(sent).astype(F32)


def folded_body(inputs, down_weight, up_weight, value_grad):
    tokens, down, up, cotangent = inputs[0], down_weight[0], up_weight[0], value_grad[0]
    rows = tokens.shape[0]
    lat = down.shape[0]
    feat = cotangent.shape[1]
    place = lax.axis_index("row")
    middle = (place == 1) | (place == 2)

    cut = feat // 2
    cuts = (slice(0, cut), slice(cut, feat))
    down_end = inward(down)
    tokens_end = inward(tokens)
    down_other = across(down)
    cot_other = across(cotangent)
    cot_end = [inward(cotangent[:, cuts[0]])]
    down_other_end = across(down_end)
    cot_end.append(inward(after(cotangent[:, cuts[1]], down_end, down_other)))
    cot_other_end = [across(cot_end[0])]
    up_end = inward(after(up, tokens_end, cot_end[0]))
    down_there = [outward(down), outward(down_other), outward(down_other_end)]

    tokens_mine = jnp.concatenate([tokens, after(tokens_end, down_there[0])], axis=0)
    down_all = jnp.concatenate([down, down_end, down_other, down_other_end], axis=0)
    down_used = jnp.where(
        middle,
        down_all,
        jnp.concatenate([down_there[0], down, down_there[1], down_there[2]], axis=0),
    )

    latent = col_sum(rows_dot(tokens_mine, down_all))
    inv_rms = lax.rsqrt(jnp.mean(latent * latent, axis=-1, keepdims=True) + 1e-06)
    normed = latent * inv_rms
    normed_bf = normed.astype(BF16)
    normed_sent = after(normed_bf[:, 2 * lat :], down_there[1])
    normed_other = across(normed_sent)
    normed_all = jnp.concatenate([normed_bf[:, : 2 * lat], normed_other], axis=0)

    cot_other_end.append(across(after(cot_end[1], normed_sent)))
    def early_rows(k):
        return jnp.concatenate([cotangent[:, cuts[k]], cot_end[k], cot_other[:, cuts[k]]], axis=0)

    values = jnp.concatenate([early_rows(0), cot_other_end[0]], axis=0)
    up_first = tokens_dot(after(normed_all, down_there[2]), values).astype(BF16)
    back_first = outward(up_first[lat:])
    up_mine = jnp.concatenate([up, after(up_end, up_first, down_used)], axis=0)
    grad = rows_dot(values, up_mine[:, cuts[0]])
    early = grad[: 3 * rows] + rows_dot(early_rows(1), up_mine[:, cuts[1]])
    early = early.astype(BF16)
    early_sum = early.astype(F32) + other_col(early).astype(F32)

    last = after(cot_other_end[1], early)
    late = col_sum(grad[3 * rows :] + rows_dot(last, up_mine[:, cuts[1]]))
    values = jnp.concatenate([early_rows(1), last], axis=0)
    up_second = tokens_dot(normed_all, values).astype(BF16)
    back_second = outward(up_second[lat:])
    grad_sent = jnp.concatenate([early_sum[2 * rows :], late], axis=0).astype(BF16)
    from_across = across(after(grad_sent, up_second, back_first))
    normed_grad = jnp.concatenate([early_sum[: 2 * rows], from_across.astype(F32)], axis=1)
    inner = jnp.mean(normed_grad * normed, axis=-1, keepdims=True)
    latent_bf = (inv_rms * (normed_grad - normed * inner)).astype(BF16)
    latent_there = outward(latent_bf[rows:])
    latent_used = jnp.where(middle, latent_bf[:rows], latent_there)

    sums = [
        tokens_dot(latent_bf[:, j * lat : (j + 1) * lat], tokens_mine).astype(BF16)
        for j in range(4)
    ]
    width = tokens.shape[1]
    first = width * 2 // 5 // 128 * 128
    halves = (slice(0, first), slice(first, width))
    sent_end, sent_own = sums[3], sums[2]
    from_end = [across(sent_end[:, half]) for half in halves]
    end_first = (sums[1][:, halves[0]] + from_end[0].astype(F32)).astype(BF16)
    from_own = across(after(sent_own, end_first))
    end_second = sums[1][:, halves[1]] + after(from_end[1], end_first).astype(F32)
    end_second = end_second.astype(BF16)
    down_end_grad = jnp.concatenate([outward(end_first), outward(end_second)], axis=1)
    up_grad = jnp.concatenate(
        [
            jnp.where(middle, up_first[:lat], back_first),
            jnp.where(middle, up_second[:lat], after(back_second, end_second)),
        ],
        axis=1,
    )

    input_grad = jnp.dot(latent_used, down_used, preferred_element_type=F32).astype(BF16)
    passed = shifted(input_grad, "section", -1)
    down_own_grad = (sums[0] + after(from_own, passed).astype(F32)).astype(BF16)
    down_grad = jnp.where(middle, down_own_grad, down_end_grad)
    return (passed[None], down_grad[None], up_grad[None])


def solution(mesh):
    spec = P("section", "row", "col")
    folds = mesh.shape["row"] == 4 and mesh.shape["col"] == 2
    return jax.shard_map(
        folded_body if folds else general_body,
        mesh=mesh,
        in_specs=(spec,) * 4,
        out_specs=(spec,) * 3,
        check_vma=False,
    )
```

```python
import jax
import jax.numpy as jnp
from jax import lax
from jax.sharding import PartitionSpec as P

F32 = jnp.float32
BF16 = jnp.bfloat16


def shifted(value, axis, steps):
    count = lax.axis_size(axis)
    leading, last = (max(0, -steps), min(count, count - steps))
    return lax.ppermute(value, axis, [(source, source + steps) for source in range(leading, last)])


def general_body(inputs, down_weight, up_weight, value_grad):
    tokens = inputs[0]
    cotangent = value_grad[0]
    down_full = lax.all_gather(down_weight[0], "row", axis=0, tiled=True)
    up_full = lax.all_gather(up_weight[0], "row", axis=0, tiled=True)
    latent_part = jnp.einsum("td,ld->tl", tokens, down_full, preferred_element_type=F32)
    grad_part = jnp.einsum("tf,lf->tl", cotangent, up_full, preferred_element_type=F32)
    latent = lax.psum(latent_part.astype(BF16), "col").astype(F32)
    normed_grad = lax.psum(grad_part.astype(BF16), "col").astype(F32)
    inv_rms = lax.rsqrt(jnp.mean(latent * latent, axis=-1, keepdims=True) + 1e-06)
    normed = latent * inv_rms
    normed_bf = normed.astype(BF16)
    inner = jnp.mean(normed_grad * normed, axis=-1, keepdims=True)
    latent_bf = (inv_rms * (normed_grad - normed * inner)).astype(BF16)
    up_grad = lax.psum_scatter(
        jnp.einsum("tl,tf->lf", normed_bf, cotangent, preferred_element_type=F32).astype(BF16),
        "row",
        scatter_dimension=0,
        tiled=True,
    )
    down_grad = lax.psum_scatter(
        jnp.einsum("tl,td->ld", latent_bf, tokens, preferred_element_type=F32).astype(BF16),
        "row",
        scatter_dimension=0,
        tiled=True,
    )
    input_grad = jnp.einsum("tl,ld->td", latent_bf, down_full, preferred_element_type=F32)
    passed = shifted(input_grad.astype(BF16), "section", -1)
    return (passed[None], down_grad[None], up_grad[None])


def inward(value):
    return lax.ppermute(value, "row", [(0, 1), (3, 2)])


def across(value):
    return lax.ppermute(value, "row", [(1, 2), (2, 1)])


def outward(value):
    return lax.ppermute(value, "row", [(1, 0), (2, 3)])


def other_col(value):
    return lax.ppermute(value, "col", [(0, 1), (1, 0)])


def after(value, *earlier):
    return lax.optimization_barrier((value, *earlier))[0]


def rows_dot(left, right):
    return lax.dot_general(left, right, (((1,), (1,)), ((), ())), preferred_element_type=F32)


def tokens_dot(left, right):
    return lax.dot_general(left, right, (((0,), (0,)), ((), ())), preferred_element_type=F32)


def col_sum(part):
    sent = part.astype(BF16)
    return sent.astype(F32) + other_col(sent).astype(F32)


def folded_body(inputs, down_weight, up_weight, value_grad):
    tokens, down, up, cotangent = inputs[0], down_weight[0], up_weight[0], value_grad[0]
    rows = tokens.shape[0]
    lat = down.shape[0]
    feat = cotangent.shape[1]
    place = lax.axis_index("row")
    middle = (place == 1) | (place == 2)

    cut = feat // 2
    cuts = (slice(0, cut), slice(cut, feat))
    down_end = inward(down)
    tokens_end = inward(tokens)
    down_other = across(down)
    cot_other = across(cotangent)
    cot_end = [inward(cotangent[:, cuts[0]])]
    down_other_end = across(down_end)
    cot_end.append(inward(after(cotangent[:, cuts[1]], down_end, down_other)))
    cot_other_end = [across(cot_end[0])]
    up_end = inward(after(up, tokens_end, cot_end[0]))
    down_there = [outward(down), outward(down_other), outward(down_other_end)]

    tokens_mine = jnp.concatenate([tokens, after(tokens_end, down_there[0])], axis=0)
    down_all = jnp.concatenate([down, down_end, down_other, down_other_end], axis=0)
    down_used = jnp.where(
        middle,
        down_all,
        jnp.concatenate([down_there[0], down, down_there[1], down_there[2]], axis=0),
    )

    latent = col_sum(rows_dot(tokens_mine, down_all))
    inv_rms = lax.rsqrt(jnp.mean(latent * latent, axis=-1, keepdims=True) + 1e-06)
    normed = latent * inv_rms
    normed_bf = normed.astype(BF16)
    normed_sent = after(normed_bf[:, 2 * lat :], down_there[1])
    normed_other = across(normed_sent)
    normed_all = jnp.concatenate([normed_bf[:, : 2 * lat], normed_other], axis=0)

    cot_other_end.append(across(after(cot_end[1], normed_sent)))
    def early_rows(k):
        return jnp.concatenate([cotangent[:, cuts[k]], cot_end[k], cot_other[:, cuts[k]]], axis=0)

    values = jnp.concatenate([early_rows(0), cot_other_end[0]], axis=0)
    up_first = tokens_dot(after(normed_all, down_there[2]), values).astype(BF16)
    back_first = outward(up_first[lat:])
    up_mine = jnp.concatenate([up, after(up_end, up_first, down_used)], axis=0)
    grad = rows_dot(values, up_mine[:, cuts[0]])
    early = grad[: 3 * rows] + rows_dot(early_rows(1), up_mine[:, cuts[1]])
    early = early.astype(BF16)
    early_sum = early.astype(F32) + other_col(early).astype(F32)

    last = after(cot_other_end[1], early)
    late = col_sum(grad[3 * rows :] + rows_dot(last, up_mine[:, cuts[1]]))
    values = jnp.concatenate([early_rows(1), last], axis=0)
    up_second = tokens_dot(normed_all, values).astype(BF16)
    back_second = outward(up_second[lat:])
    grad_sent = jnp.concatenate([early_sum[2 * rows :], late], axis=0).astype(BF16)
    from_across = across(after(grad_sent, up_second, back_first))
    normed_grad = jnp.concatenate([early_sum[: 2 * rows], from_across.astype(F32)], axis=1)
    inner = jnp.mean(normed_grad * normed, axis=-1, keepdims=True)
    latent_bf = (inv_rms * (normed_grad - normed * inner)).astype(BF16)
    latent_there = outward(latent_bf[rows:])
    latent_used = jnp.where(middle, latent_bf[:rows], latent_there)

    sums = [
        tokens_dot(latent_bf[:, j * lat : (j + 1) * lat], tokens_mine).astype(BF16)
        for j in range(4)
    ]
    width = tokens.shape[1]
    first = width * 3 // 10 // 128 * 128
    halves = (slice(0, first), slice(first, width))
    sent_end, sent_own = sums[3], sums[2]
    from_end = [across(sent_end[:, half]) for half in halves]
    end_first = (sums[1][:, halves[0]] + from_end[0].astype(F32)).astype(BF16)
    from_own = across(after(sent_own, end_first))
    end_second = sums[1][:, halves[1]] + after(from_end[1], end_first).astype(F32)
    end_second = end_second.astype(BF16)
    down_end_grad = jnp.concatenate([outward(end_first), outward(end_second)], axis=1)
    up_grad = jnp.concatenate(
        [
            jnp.where(middle, up_first[:lat], back_first),
            jnp.where(middle, up_second[:lat], after(back_second, end_second)),
        ],
        axis=1,
    )

    input_grad = jnp.dot(latent_used, down_used, preferred_element_type=F32).astype(BF16)
    passed = shifted(input_grad, "section", -1)
    down_own_grad = (sums[0] + after(from_own, passed).astype(F32)).astype(BF16)
    down_grad = jnp.where(middle, down_own_grad, down_end_grad)
    return (passed[None], down_grad[None], up_grad[None])


def solution(mesh):
    spec = P("section", "row", "col")
    folds = mesh.shape["row"] == 4 and mesh.shape["col"] == 2
    return jax.shard_map(
        folded_body if folds else general_body,
        mesh=mesh,
        in_specs=(spec,) * 4,
        out_specs=(spec,) * 3,
        check_vma=False,
    )
```

```python
import jax
import jax.numpy as jnp
from jax import lax
from jax.sharding import PartitionSpec as P

F32 = jnp.float32
BF16 = jnp.bfloat16


def shifted(value, axis, steps):
    count = lax.axis_size(axis)
    leading, last = (max(0, -steps), min(count, count - steps))
    return lax.ppermute(value, axis, [(source, source + steps) for source in range(leading, last)])


def general_body(inputs, down_weight, up_weight, value_grad):
    tokens = inputs[0]
    cotangent = value_grad[0]
    down_full = lax.all_gather(down_weight[0], "row", axis=0, tiled=True)
    up_full = lax.all_gather(up_weight[0], "row", axis=0, tiled=True)
    latent_part = jnp.einsum("td,ld->tl", tokens, down_full, preferred_element_type=F32)
    grad_part = jnp.einsum("tf,lf->tl", cotangent, up_full, preferred_element_type=F32)
    latent = lax.psum(latent_part.astype(BF16), "col").astype(F32)
    normed_grad = lax.psum(grad_part.astype(BF16), "col").astype(F32)
    inv_rms = lax.rsqrt(jnp.mean(latent * latent, axis=-1, keepdims=True) + 1e-06)
    normed = latent * inv_rms
    normed_bf = normed.astype(BF16)
    inner = jnp.mean(normed_grad * normed, axis=-1, keepdims=True)
    latent_bf = (inv_rms * (normed_grad - normed * inner)).astype(BF16)
    up_grad = lax.psum_scatter(
        jnp.einsum("tl,tf->lf", normed_bf, cotangent, preferred_element_type=F32).astype(BF16),
        "row",
        scatter_dimension=0,
        tiled=True,
    )
    down_grad = lax.psum_scatter(
        jnp.einsum("tl,td->ld", latent_bf, tokens, preferred_element_type=F32).astype(BF16),
        "row",
        scatter_dimension=0,
        tiled=True,
    )
    input_grad = jnp.einsum("tl,ld->td", latent_bf, down_full, preferred_element_type=F32)
    passed = shifted(input_grad.astype(BF16), "section", -1)
    return (passed[None], down_grad[None], up_grad[None])


def inward(value):
    return lax.ppermute(value, "row", [(0, 1), (3, 2)])


def across(value):
    return lax.ppermute(value, "row", [(1, 2), (2, 1)])


def outward(value):
    return lax.ppermute(value, "row", [(1, 0), (2, 3)])


def other_col(value):
    return lax.ppermute(value, "col", [(0, 1), (1, 0)])


def after(value, *earlier):
    return lax.optimization_barrier((value, *earlier))[0]


def rows_dot(left, right):
    return lax.dot_general(left, right, (((1,), (1,)), ((), ())), preferred_element_type=F32)


def tokens_dot(left, right):
    return lax.dot_general(left, right, (((0,), (0,)), ((), ())), preferred_element_type=F32)


def col_sum(part):
    sent = part.astype(BF16)
    return sent.astype(F32) + other_col(sent).astype(F32)


def folded_body(inputs, down_weight, up_weight, value_grad):
    tokens, down, up, cotangent = inputs[0], down_weight[0], up_weight[0], value_grad[0]
    rows = tokens.shape[0]
    lat = down.shape[0]
    feat = cotangent.shape[1]
    place = lax.axis_index("row")
    middle = (place == 1) | (place == 2)

    cut = feat * 5 // 8 // 128 * 128
    cuts = (slice(0, cut), slice(cut, feat))
    down_end = inward(down)
    tokens_end = inward(tokens)
    down_other = across(down)
    cot_other = across(cotangent)
    cot_end = [inward(cotangent[:, cuts[0]])]
    down_other_end = across(down_end)
    cot_end.append(inward(after(cotangent[:, cuts[1]], down_end, down_other)))
    cot_other_end = [across(cot_end[0])]
    up_end = inward(after(up, tokens_end, cot_end[0]))
    down_there = [outward(down), outward(down_other), outward(down_other_end)]

    tokens_mine = jnp.concatenate([tokens, after(tokens_end, down_there[0])], axis=0)
    down_all = jnp.concatenate([down, down_end, down_other, down_other_end], axis=0)
    down_used = jnp.where(
        middle,
        down_all,
        jnp.concatenate([down_there[0], down, down_there[1], down_there[2]], axis=0),
    )

    latent = col_sum(rows_dot(tokens_mine, down_all))
    inv_rms = lax.rsqrt(jnp.mean(latent * latent, axis=-1, keepdims=True) + 1e-06)
    normed = latent * inv_rms
    normed_bf = normed.astype(BF16)
    normed_sent = after(normed_bf[:, 2 * lat :], down_there[1])
    normed_other = across(normed_sent)
    normed_all = jnp.concatenate([normed_bf[:, : 2 * lat], normed_other], axis=0)

    cot_other_end.append(across(after(cot_end[1], normed_sent)))
    def early_rows(k):
        return jnp.concatenate([cotangent[:, cuts[k]], cot_end[k], cot_other[:, cuts[k]]], axis=0)

    values = jnp.concatenate([early_rows(0), cot_other_end[0]], axis=0)
    up_first = tokens_dot(after(normed_all, down_there[2]), values).astype(BF16)
    back_first = outward(up_first[lat:])
    up_mine = jnp.concatenate([up, after(up_end, up_first, down_used)], axis=0)
    grad = rows_dot(values, up_mine[:, cuts[0]])
    early = grad[: 3 * rows] + rows_dot(early_rows(1), up_mine[:, cuts[1]])
    early = early.astype(BF16)
    early_sum = early.astype(F32) + other_col(early).astype(F32)

    last = after(cot_other_end[1], early)
    late = col_sum(grad[3 * rows :] + rows_dot(last, up_mine[:, cuts[1]]))
    values = jnp.concatenate([early_rows(1), last], axis=0)
    up_second = tokens_dot(normed_all, values).astype(BF16)
    back_second = outward(up_second[lat:])
    grad_sent = jnp.concatenate([early_sum[2 * rows :], late], axis=0).astype(BF16)
    from_across = across(after(grad_sent, up_second, back_first))
    normed_grad = jnp.concatenate([early_sum[: 2 * rows], from_across.astype(F32)], axis=1)
    inner = jnp.mean(normed_grad * normed, axis=-1, keepdims=True)
    latent_bf = (inv_rms * (normed_grad - normed * inner)).astype(BF16)
    latent_there = outward(latent_bf[rows:])
    latent_used = jnp.where(middle, latent_bf[:rows], latent_there)

    sums = [
        tokens_dot(latent_bf[:, j * lat : (j + 1) * lat], tokens_mine).astype(BF16)
        for j in range(4)
    ]
    width = tokens.shape[1]
    first = width * 2 // 5 // 128 * 128
    halves = (slice(0, first), slice(first, width))
    sent_end, sent_own = sums[3], sums[2]
    from_end = [across(sent_end[:, half]) for half in halves]
    end_first = (sums[1][:, halves[0]] + from_end[0].astype(F32)).astype(BF16)
    from_own = across(after(sent_own, end_first))
    end_second = sums[1][:, halves[1]] + after(from_end[1], end_first).astype(F32)
    end_second = end_second.astype(BF16)
    down_end_grad = jnp.concatenate([outward(end_first), outward(end_second)], axis=1)
    up_grad = jnp.concatenate(
        [
            jnp.where(middle, up_first[:lat], back_first),
            jnp.where(middle, up_second[:lat], after(back_second, end_second)),
        ],
        axis=1,
    )

    input_grad = jnp.dot(latent_used, down_used, preferred_element_type=F32).astype(BF16)
    passed = shifted(input_grad, "section", -1)
    down_own_grad = (sums[0] + after(from_own, passed).astype(F32)).astype(BF16)
    down_grad = jnp.where(middle, down_own_grad, down_end_grad)
    return (passed[None], down_grad[None], up_grad[None])


def solution(mesh):
    spec = P("section", "row", "col")
    folds = mesh.shape["row"] == 4 and mesh.shape["col"] == 2
    return jax.shard_map(
        folded_body if folds else general_body,
        mesh=mesh,
        in_specs=(spec,) * 4,
        out_specs=(spec,) * 3,
        check_vma=False,
    )
```

```python
import jax
import jax.numpy as jnp
from jax import lax
from jax.sharding import PartitionSpec as P

F32 = jnp.float32
BF16 = jnp.bfloat16


def shifted(value, axis, steps):
    count = lax.axis_size(axis)
    leading, last = (max(0, -steps), min(count, count - steps))
    return lax.ppermute(value, axis, [(source, source + steps) for source in range(leading, last)])


def general_body(inputs, down_weight, up_weight, value_grad):
    tokens = inputs[0]
    cotangent = value_grad[0]
    down_full = lax.all_gather(down_weight[0], "row", axis=0, tiled=True)
    up_full = lax.all_gather(up_weight[0], "row", axis=0, tiled=True)
    latent_part = jnp.einsum("td,ld->tl", tokens, down_full, preferred_element_type=F32)
    grad_part = jnp.einsum("tf,lf->tl", cotangent, up_full, preferred_element_type=F32)
    latent = lax.psum(latent_part.astype(BF16), "col").astype(F32)
    normed_grad = lax.psum(grad_part.astype(BF16), "col").astype(F32)
    inv_rms = lax.rsqrt(jnp.mean(latent * latent, axis=-1, keepdims=True) + 1e-06)
    normed = latent * inv_rms
    normed_bf = normed.astype(BF16)
    inner = jnp.mean(normed_grad * normed, axis=-1, keepdims=True)
    latent_bf = (inv_rms * (normed_grad - normed * inner)).astype(BF16)
    up_grad = lax.psum_scatter(
        jnp.einsum("tl,tf->lf", normed_bf, cotangent, preferred_element_type=F32).astype(BF16),
        "row",
        scatter_dimension=0,
        tiled=True,
    )
    down_grad = lax.psum_scatter(
        jnp.einsum("tl,td->ld", latent_bf, tokens, preferred_element_type=F32).astype(BF16),
        "row",
        scatter_dimension=0,
        tiled=True,
    )
    input_grad = jnp.einsum("tl,ld->td", latent_bf, down_full, preferred_element_type=F32)
    passed = shifted(input_grad.astype(BF16), "section", -1)
    return (passed[None], down_grad[None], up_grad[None])


def inward(value):
    return lax.ppermute(value, "row", [(0, 1), (3, 2)])


def across(value):
    return lax.ppermute(value, "row", [(1, 2), (2, 1)])


def outward(value):
    return lax.ppermute(value, "row", [(1, 0), (2, 3)])


def other_col(value):
    return lax.ppermute(value, "col", [(0, 1), (1, 0)])


def after(value, *earlier):
    return lax.optimization_barrier((value, *earlier))[0]


def rows_dot(left, right):
    return lax.dot_general(left, right, (((1,), (1,)), ((), ())), preferred_element_type=F32)


def tokens_dot(left, right):
    return lax.dot_general(left, right, (((0,), (0,)), ((), ())), preferred_element_type=F32)


def col_sum(part):
    sent = part.astype(BF16)
    return sent.astype(F32) + other_col(sent).astype(F32)


def folded_body(inputs, down_weight, up_weight, value_grad):
    tokens, down, up, cotangent = inputs[0], down_weight[0], up_weight[0], value_grad[0]
    rows = tokens.shape[0]
    lat = down.shape[0]
    feat = cotangent.shape[1]
    place = lax.axis_index("row")
    middle = (place == 1) | (place == 2)

    cut = feat // 2
    cuts = (slice(0, cut), slice(cut, feat))
    down_end = inward(down)
    tokens_end = inward(tokens)
    down_other = across(down)
    cot_other = across(cotangent)
    cot_end = [inward(cotangent[:, cuts[0]])]
    down_other_end = across(down_end)
    cot_end.append(inward(after(cotangent[:, cuts[1]], down_end, down_other)))
    cot_other_end = [across(cot_end[0])]
    up_end = inward(after(up, tokens_end, cot_end[0]))
    down_there = [outward(down), outward(down_other), outward(down_other_end)]

    tokens_mine = jnp.concatenate([tokens, after(tokens_end, down_there[0])], axis=0)
    down_all = jnp.concatenate([down, down_end, down_other, down_other_end], axis=0)
    down_used = jnp.where(
        middle,
        down_all,
        jnp.concatenate([down_there[0], down, down_there[1], down_there[2]], axis=0),
    )

    latent = col_sum(rows_dot(tokens_mine, down_all))
    inv_rms = lax.rsqrt(jnp.mean(latent * latent, axis=-1, keepdims=True) + 1e-06)
    normed = latent * inv_rms
    normed_bf = normed.astype(BF16)
    normed_sent = after(normed_bf[:, 2 * lat :], down_there[1])
    normed_other = across(normed_sent)
    normed_all = jnp.concatenate([normed_bf[:, : 2 * lat], normed_other], axis=0)

    cot_other_end.append(across(after(cot_end[1], normed_sent)))
    def early_rows(k):
        return jnp.concatenate([cotangent[:, cuts[k]], cot_end[k], cot_other[:, cuts[k]]], axis=0)

    values = jnp.concatenate([early_rows(0), cot_other_end[0]], axis=0)
    up_first = tokens_dot(after(normed_all, down_there[2]), values).astype(BF16)
    back_first = outward(up_first[lat:])
    up_mine = jnp.concatenate([up, after(up_end, up_first, down_used)], axis=0)
    grad = rows_dot(values, up_mine[:, cuts[0]])
    early = grad[: 3 * rows] + rows_dot(early_rows(1), up_mine[:, cuts[1]])
    early = early.astype(BF16)
    early_sum = early.astype(F32) + other_col(early).astype(F32)

    last = after(cot_other_end[1], early)
    late = col_sum(grad[3 * rows :] + rows_dot(last, up_mine[:, cuts[1]]))
    values = jnp.concatenate([early_rows(1), last], axis=0)
    up_second = tokens_dot(normed_all, values).astype(BF16)
    back_second = outward(up_second[lat:])
    grad_sent = jnp.concatenate([early_sum[2 * rows :], late], axis=0).astype(BF16)
    from_across = across(after(grad_sent, up_second, back_first))
    normed_grad = jnp.concatenate([early_sum[: 2 * rows], from_across.astype(F32)], axis=1)
    inner = jnp.mean(normed_grad * normed, axis=-1, keepdims=True)
    latent_bf = (inv_rms * (normed_grad - normed * inner)).astype(BF16)
    latent_there = outward(latent_bf[rows:])
    latent_used = jnp.where(middle, latent_bf[:rows], latent_there)

    sent_end = tokens_dot(latent_bf[:, 3 * lat :], tokens_mine).astype(BF16)
    latent_late = after(latent_bf, latent_there)
    sums = [
        tokens_dot(latent_late[:, j * lat : (j + 1) * lat], tokens_mine).astype(BF16)
        for j in range(3)
    ]
    width = tokens.shape[1]
    first = width * 2 // 5 // 128 * 128
    halves = (slice(0, first), slice(first, width))
    sent_own = sums[2]
    from_end = [across(sent_end[:, half]) for half in halves]
    end_first = (sums[1][:, halves[0]] + from_end[0].astype(F32)).astype(BF16)
    from_own = across(after(sent_own, end_first))
    end_second = sums[1][:, halves[1]] + after(from_end[1], end_first).astype(F32)
    end_second = end_second.astype(BF16)
    down_end_grad = jnp.concatenate([outward(end_first), outward(end_second)], axis=1)
    up_grad = jnp.concatenate(
        [
            jnp.where(middle, up_first[:lat], back_first),
            jnp.where(middle, up_second[:lat], after(back_second, end_second)),
        ],
        axis=1,
    )

    input_grad = jnp.dot(latent_used, down_used, preferred_element_type=F32).astype(BF16)
    passed = shifted(input_grad, "section", -1)
    down_own_grad = (sums[0] + after(from_own, passed).astype(F32)).astype(BF16)
    down_grad = jnp.where(middle, down_own_grad, down_end_grad)
    return (passed[None], down_grad[None], up_grad[None])


def solution(mesh):
    spec = P("section", "row", "col")
    folds = mesh.shape["row"] == 4 and mesh.shape["col"] == 2
    return jax.shard_map(
        folded_body if folds else general_body,
        mesh=mesh,
        in_specs=(spec,) * 4,
        out_specs=(spec,) * 3,
        check_vma=False,
    )
```
